256 devices in a mesh: store: 32 (over y, z), head: 4 (over x), rep: 2 (over core).
Axes of the slice: x: 4, y: 4, z: 8, core: 2. Of those that a mesh axis runs over, the one named last changes fastest.
Arguments:
- queries: bfloat16 [64, 128, 8192], P(('store', 'rep'), None, 'head'), may hold values from -168 to 168
- span_keys: bfloat16 [64, 128, 1024], P(('store', 'rep'), None, 'head'), may hold values from -12 to 12
- span_values: bfloat16 [64, 128, 1024], P(('store', 'rep'), None, 'head'), may hold values from -6 to 6
- page_cache: bfloat16 [256, 2, 256, 1024], P('store', None, None, 'head'), may hold values from -8.5 to 8.5
- passage_ids: int32 [64, 8], P(('store', 'rep')), may hold values from 0 to 255, as said below
- starts: int32 [64, 8], P(('store', 'rep')), may hold values from 0 to 2815, as said below
- out_weight: bfloat16 [8192, 4, 2, 512], P('head', None, 'rep'), may hold values from -0.59765625 to 0.59765625
Outputs:
- layer_output: bfloat16 [64, 128, 4096], P(('store', 'rep'), None, 'head')
The draws below stay inside these ranges and needn't reach their ends.
Inputs may be any that keep to these rules, and one draw needn't show every extreme that they name: `passage_ids`: each request names 8 different passages; passage p is held by index p // 8 of store, and at most 1 passages of one request share an index. A request's starts are its own offset plus 256 times a permutation of 0 to 7.
All inputs are finite; a program needn't handle non-finite values.
Results may differ from the reference program's by a relative error of at most 0.012.
The reference program's roundings to bfloat16 on the way count: a program that leaves them out, or rounds other values in their place, can miss the bound.
Values may be sent and summed in bfloat16 or wider, within the bound.
No kernel may reach another device: no remote copies, remote signals or barrier semaphores. Data moves between devices by JAX's collectives and lax.ppermute only.
A program may use at most 128 MiB of HBM per device.

```python
import math
import jax
import jax.numpy as jnp
from jax import lax

HQ = 64
KVH = 8
HD = 128
DW = 4096
PAGE = 256
NPASS = 8
Q = 128
P_DEV = 8
R = 64
CAP = 1
CB = 512
PASSAGES = 256
N_HEAD = 4
N_REP = 2


def joint_parts(key):
    normal_part = jnp.clip(jax.random.normal(jax.random.fold_in(key, 11), (R, Q, KVH, HD), jnp.float32), -4.0, 4.0)
    return normal_part


def draw_queries(key, part):
    key = jax.random.fold_in(key, 1)
    values = 2.0 * jnp.clip(jax.random.normal(key, (R, Q, HQ, HD), jnp.float32), -4.0, 4.0)
    return values.reshape(R, Q, HQ * HD).astype(jnp.bfloat16)


def draw_span_keys(key, part):
    normal_part = joint_parts(key)
    values = 1.5 * normal_part
    return values.reshape(R, Q, KVH * HD).astype(jnp.bfloat16)


def draw_page_cache(key, part):
    key = jax.random.fold_in(key, 3)
    full_shape = (PASSAGES, 2, PAGE, KVH * HD)
    values = jnp.clip(jax.random.normal(key, full_shape, jnp.float32), -4.0, 4.0)
    return values.astype(jnp.bfloat16)


def draw_passage_ids(key, part):
    key = jax.random.fold_in(key, 4)
    store_count = PASSAGES // P_DEV
    bin_count = store_count * CAP
    store_weight = jax.random.randint(jax.random.fold_in(key, 1), (store_count,), 1, 9)
    bin_weight = jnp.repeat(store_weight, CAP)
    raw_scores = jax.random.randint(jax.random.fold_in(key, 2), (R, bin_count), 0, 1024)
    scores = raw_scores * bin_weight[None, :] * bin_count + jnp.arange(bin_count, dtype=jnp.int32)[None, :]
    best_scores, chosen = lax.top_k(scores, NPASS)
    owners = chosen // CAP
    sub_slot = chosen % CAP
    spread = P_DEV // CAP
    offset = jax.random.randint(jax.random.fold_in(key, 3), (R, NPASS), 0, spread)
    return (owners * P_DEV + sub_slot * spread + offset).astype(jnp.int32)


def draw_starts(key, part):
    key = jax.random.fold_in(key, 5)
    row_keys = jax.random.split(jax.random.fold_in(key, 1), R)

    def permute_row(row_key):
        return jax.random.permutation(row_key, NPASS)
    orders = jax.vmap(permute_row)(row_keys)
    prefix = jax.random.randint(jax.random.fold_in(key, 2), (R,), 0, 1024)
    prefix = prefix.at[0].set(1023).at[R - 1].set(0)
    return (prefix[:, None] + PAGE * orders).astype(jnp.int32)


def level_of(key, extent, cuts, least, high):
    loudness, own = 1.0, jax.random.fold_in(key, 6)
    for axis_at, blocks in cuts:
        heights = jnp.exp(jax.random.uniform(jax.random.fold_in(own, axis_at), (blocks,), jnp.float32, least / len(cuts), high / len(cuts)))
        loudness = loudness * jnp.repeat(heights, extent[axis_at] // blocks).reshape([-1 if axis == axis_at else 1 for axis in range(len(extent))])
    return loudness


def centred(rng, dims, deviation, bound, cuts=(), kind=jnp.bfloat16):
    values = deviation * jax.random.normal(rng, dims, jnp.float32)
    if cuts:
        values = values * level_of(rng, dims, cuts, -0.22, 0.18)
    return jnp.clip(values, -bound, bound).astype(kind)


def setup_inputs(seed: int = 0) -> dict:
    key_list = jax.random.split(jax.random.key(seed), 8)
    queries = draw_queries(jax.random.fold_in(key_list[7], 71), 0)
    span_keys = draw_span_keys(jax.random.fold_in(key_list[7], 71), 0)
    span_values = centred(key_list[2], (R, Q, KVH * HD), 1.0, 6.0, ((0, 64), (2, 4)))
    page_cache = draw_page_cache(jax.random.fold_in(key_list[7], 71), 0)
    passage_ids = draw_passage_ids(jax.random.fold_in(key_list[7], 71), 0)
    starts = draw_starts(jax.random.fold_in(key_list[7], 71), 0)
    out_weight = centred(key_list[6], (HQ * HD, N_HEAD, N_REP, CB), 0.1, 0.59765625, ((0, 4), (2, 2)))
    return {"queries": queries, "span_keys": span_keys, "span_values": span_values, "page_cache": page_cache, "passage_ids": passage_ids, "starts": starts, "out_weight": out_weight}


theta_base = 1000000.0

def rotate(values, positions):
    half_dim = values.shape[-1] // 2
    inverse_freq = jnp.exp(-(2.0 * jnp.arange(half_dim, dtype=jnp.float32) / values.shape[-1]) * math.log(theta_base))
    angles = positions.astype(jnp.float32)[..., None] * inverse_freq
    cosine = jnp.cos(angles)
    sine_part = jnp.sin(angles)
    first_half = values[..., :half_dim]
    second = values[..., half_dim:]
    return jnp.concatenate([first_half * cosine - second * sine_part, second * cosine + first_half * sine_part], axis=-1)

def reference(queries, span_keys, span_values, page_cache, passage_ids, starts, out_weight):
    group_size = HQ // KVH
    score_scale = 1.0 / math.sqrt(HD)
    flat_weight = out_weight.reshape(HQ * HD, DW)

    def one_request(request_args):
        query_rows, key_rows, value_rows, passage_list, begins = request_args
        query_start = jnp.min(begins) + NPASS * PAGE
        query_pos = query_start + jnp.arange(Q, dtype=jnp.int32)
        query_rot = rotate(query_rows.reshape(Q, HQ, HD).astype(jnp.float32), query_pos[:, None]).astype(jnp.bfloat16)
        near_keys = rotate(key_rows.reshape(Q, KVH, HD).astype(jnp.float32), query_pos[:, None]).astype(jnp.bfloat16)
        near_values = value_rows.reshape(Q, KVH, HD)
        fetched = page_cache[passage_list]
        page_pos = begins[:, None] + jnp.arange(PAGE, dtype=jnp.int32)[None, :]
        far_keys = rotate(fetched[:, 0].reshape(NPASS, PAGE, KVH, HD).astype(jnp.float32), page_pos[:, :, None])
        far_keys = far_keys.astype(jnp.bfloat16).reshape(NPASS * PAGE, KVH, HD)
        far_values = fetched[:, 1].reshape(NPASS * PAGE, KVH, HD)
        query_group = query_rot.reshape(Q, KVH, group_size, HD).astype(jnp.float32)
        far_scores = jnp.einsum('qhgd,khd->hgqk', query_group, far_keys.astype(jnp.float32)) * score_scale
        near_scores = jnp.einsum('qhgd,khd->hgqk', query_group, near_keys.astype(jnp.float32)) * score_scale
        allowed = jnp.arange(Q)[:, None] >= jnp.arange(Q)[None, :]
        near_scores = jnp.where(allowed, near_scores, -jnp.inf)
        row_max = jnp.maximum(lax.optimization_barrier(jnp.max(far_scores, axis=-1)), lax.optimization_barrier(jnp.max(near_scores, axis=-1)))[..., None]
        far_weights = jnp.exp(far_scores - row_max)
        near_weights = jnp.exp(near_scores - row_max)
        totals = lax.optimization_barrier(jnp.sum(far_weights, axis=-1)) + lax.optimization_barrier(jnp.sum(near_weights, axis=-1))
        far_rounded = lax.optimization_barrier(far_weights.astype(jnp.bfloat16)).astype(jnp.float32)
        near_rounded = lax.optimization_barrier(near_weights.astype(jnp.bfloat16)).astype(jnp.float32)
        weighted = jnp.einsum('hgqk,khd->qhgd', far_rounded, far_values.astype(jnp.float32))
        weighted = weighted + jnp.einsum('hgqk,khd->qhgd', near_rounded, near_values.astype(jnp.float32))
        attention = (weighted / jnp.transpose(totals, (2, 0, 1))[..., None]).astype(jnp.bfloat16).reshape(Q, HQ * HD)
        return jnp.dot(attention, flat_weight, preferred_element_type=jnp.float32).astype(jnp.bfloat16)
    return lax.map(one_request, (queries, span_keys, span_values, passage_ids, starts))
```

```python
import functools
import math

import jax
import jax.numpy as jnp
from jax import lax
from jax.experimental import pallas as pl
from jax.experimental.pallas import tpu as pltpu
from jax.sharding import PartitionSpec as P

HD = 128
BLK = 16
THETA = 1000000.0
SWAP = [(0, 1), (1, 0)]


def angle_tables(positions):
    half = HD // 2
    inverse_freq = jnp.exp(
        -(2.0 * jnp.arange(half, dtype=jnp.float32) / HD) * math.log(THETA)
    )
    angles = positions.astype(jnp.float32)[..., None] * inverse_freq
    cosine, sine = jnp.cos(angles), jnp.sin(angles)
    return (
        jnp.concatenate([cosine, cosine], axis=-1),
        jnp.concatenate([-sine, sine], axis=-1),
    )


def turn(x, cosine, sine):
    x = x.astype(jnp.float32)
    other = jnp.concatenate([x[:, HD // 2 :], x[:, : HD // 2]], axis=1)
    return (x * cosine + other * sine).astype(jnp.bfloat16)


def select_kernel(ids_ref, held_ref, out_ref, *, request):
    def step(dest, carry):
        for slot in range(ids_ref.shape[1]):
            out_ref[dest, slot] = held_ref[ids_ref[2 * dest + request, slot]]
        return carry

    lax.fori_loop(0, out_ref.shape[0], step, 0, unroll=4)


def select(ids, held, request):
    dests, slots = ids.shape[0] // 2, ids.shape[1]
    return pl.pallas_call(
        functools.partial(select_kernel, request=request),
        out_shape=jax.ShapeDtypeStruct((dests, slots, BLK, HD), jnp.bfloat16),
        in_specs=[
            pl.BlockSpec(memory_space=pltpu.SMEM),
            pl.BlockSpec(memory_space=pltpu.VMEM),
        ],
        out_specs=pl.BlockSpec(memory_space=pltpu.VMEM),
        cost_estimate=pl.CostEstimate(flops=0, bytes_accessed=4 << 20, transcendentals=0),
        name=f"select{request}",
    )(ids, held)


def rope_kernel(x_ref, cos_ref, sin_ref, out_ref):
    for part in range(out_ref.shape[0]):
        out_ref[part] = turn(x_ref[:, part * HD : (part + 1) * HD], cos_ref[...], sin_ref[...])


def rope_heads(rows, cosine, sine):
    tokens, width = rows.shape
    return pl.pallas_call(
        rope_kernel,
        out_shape=jax.ShapeDtypeStruct((width // HD, tokens, HD), jnp.bfloat16),
        name="rope_heads",
    )(rows, cosine, sine)


def attention_kernel(
    q_ref, near_v_ref, far_ref, cos_ref, sin_ref, out_ref, key_ref, *, group, heads
):
    tokens = near_v_ref.shape[0]
    far_len = key_ref.shape[0]
    blocks = far_ref.shape[0] // 2
    key_ref[...] = turn(
        far_ref[:blocks].reshape(far_len, HD), cos_ref[...], sin_ref[...]
    )
    far_v = far_ref[blocks:].reshape(far_len, HD)
    near_k = q_ref[heads]
    near_v = near_v_ref[...]
    rows = group * tokens
    shape = (group, tokens, tokens)
    allowed = (
        lax.broadcasted_iota(jnp.int32, shape, 1) >= lax.broadcasted_iota(jnp.int32, shape, 2)
    ).reshape(rows, tokens)
    factor = math.log2(math.e) / math.sqrt(HD)
    contract = (((1,), (1,)), ((), ()))
    for first in range(0, heads, group):
        q = q_ref[first : first + group].reshape(rows, HD)
        far_s = lax.dot_general(q, key_ref[...], contract, preferred_element_type=jnp.float32)
        near_s = lax.dot_general(q, near_k, contract, preferred_element_type=jnp.float32)
        near_s = jnp.where(allowed, near_s, -jnp.inf)
        row_max = jnp.maximum(
            jnp.max(far_s, axis=1, keepdims=True), jnp.max(near_s, axis=1, keepdims=True)
        )
        far_w = jnp.exp2((far_s - row_max) * factor)
        near_w = jnp.exp2((near_s - row_max) * factor)
        totals = jnp.sum(far_w, axis=1, keepdims=True) + jnp.sum(near_w, axis=1, keepdims=True)
        mixed = jnp.dot(far_w.astype(jnp.bfloat16), far_v, preferred_element_type=jnp.float32)
        mixed = mixed + jnp.dot(
            near_w.astype(jnp.bfloat16), near_v, preferred_element_type=jnp.float32
        )
        done = (mixed / totals).astype(jnp.bfloat16)
        for part in range(group):
            out_ref[:, (first + part) * HD : (first + part + 1) * HD] = done[
                part * tokens : (part + 1) * tokens
            ]


def attend(q_and_key, near_v, far, cosine, sine, request):
    heads = q_and_key.shape[0] - 1
    tokens = near_v.shape[0]
    far_len = cosine.shape[0]
    return pl.pallas_call(
        functools.partial(attention_kernel, group=2, heads=heads),
        out_shape=jax.ShapeDtypeStruct((tokens, heads * HD), jnp.bfloat16),
        scratch_shapes=[pltpu.VMEM((far_len, HD), jnp.bfloat16)],
        compiler_params=pltpu.CompilerParams(vmem_limit_bytes=40 << 20),
        cost_estimate=pl.CostEstimate(
            flops=4 * heads * tokens * (far_len + tokens) * HD,
            bytes_accessed=4 << 20,
            transcendentals=heads * tokens * (far_len + tokens),
        ),
        name=f"attend{request}",
    )(q_and_key, near_v, far, cosine, sine)


def on_device(queries, span_keys, span_values, page_cache, passage_ids, starts, out_weight):
    stores = lax.axis_size("store")
    rep = lax.axis_index("rep")
    per_store, _, page_len, row_width = page_cache.shape
    pass_count = passage_ids.shape[1]
    tokens = queries.shape[1]
    half_width = queries.shape[2] // 2
    page_blocks = page_len // BLK

    both = jnp.concatenate([passage_ids, starts], axis=1)
    everyone = lax.all_to_all(
        jnp.broadcast_to(both, (2 * stores, 2 * pass_count)), ("store", "rep"), 0, 0, tiled=True
    )
    ids = everyone[:, :pass_count]

    own_head = lax.dynamic_slice_in_dim(page_cache, rep * HD, HD, axis=3)
    slices = own_head.reshape(per_store, 2, page_blocks, BLK, HD).transpose(1, 2, 0, 3, 4)
    held = lax.all_to_all(
        slices.reshape(stores, per_store, BLK, HD), "store", 0, 0, tiled=True
    ).reshape(stores * per_store, BLK, HD)

    far = [
        lax.all_to_all(select(ids, held, request), "store", 0, 0, tiled=True)
        for request in range(2)
    ]


    def head_part(which):
        return jnp.concatenate(
            [
                lax.dynamic_slice_in_dim(queries[0], which * half_width, half_width, axis=1),
                lax.dynamic_slice_in_dim(span_keys[0], which * HD, HD, axis=1),
                lax.dynamic_slice_in_dim(span_values[0], which * HD, HD, axis=1),
            ],
            axis=1,
        )

    kept = head_part(rep)
    swapped = lax.ppermute(head_part(1 - rep), "rep", SWAP)
    spans = [jnp.where(rep == 0, kept, swapped), jnp.where(rep == 0, swapped, kept)]
    own_store = lax.axis_index("store")
    chip_starts = lax.dynamic_slice_in_dim(everyone, 2 * own_store, 2, axis=0)[:, pass_count:]

    weight = out_weight[:, :, 0, :].transpose(1, 0, 2)
    head_count = weight.shape[0]
    block = jnp.arange(page_blocks, dtype=jnp.int32)[:, None, None] * BLK
    token = jnp.arange(BLK, dtype=jnp.int32)[None, None, :]
    results = []
    for request in range(2):
        begins = chip_starts[request]
        query_pos = jnp.min(begins) + pass_count * page_len + jnp.arange(tokens, dtype=jnp.int32)
        rotated = rope_heads(spans[request][:, : half_width + HD], *angle_tables(query_pos))
        far_pos = (block + token + begins[None, :, None]).reshape(-1)
        own_att = attend(
            rotated, spans[request][:, half_width + HD :], far[request],
            *angle_tables(far_pos), request,
        )
        other_att = lax.ppermute(own_att, "rep", SWAP)
        att = jnp.where(
            rep == 0,
            jnp.concatenate([own_att, other_att], axis=1),
            jnp.concatenate([other_att, own_att], axis=1),
        )
        partial = jnp.einsum("tk,hkn->htn", att, weight, preferred_element_type=jnp.float32)
        parts = lax.all_to_all(partial.astype(jnp.bfloat16), "head", 0, 0, tiled=True)
        results.append(jnp.sum(parts.astype(jnp.float32), axis=0).astype(jnp.bfloat16))

    mine = jnp.where(rep == 0, results[0], results[1])
    to_zero = lax.ppermute(results[0], "rep", [(1, 0)])
    to_one = lax.ppermute(results[1], "rep", [(0, 1)])
    other = jnp.where(rep == 0, to_zero, to_one)
    return jnp.where(
        rep == 0,
        jnp.concatenate([mine, other], axis=1),
        jnp.concatenate([other, mine], axis=1),
    )[None]


def solution(mesh):
    return jax.shard_map(
        on_device,
        mesh=mesh,
        in_specs=(
            P(("store", "rep"), None, "head"),
            P(("store", "rep"), None, "head"),
            P(("store", "rep"), None, "head"),
            P("store", None, None, "head"),
            P(("store", "rep"), None),
            P(("store", "rep"), None),
            P("head", None, "rep", None),
        ),
        out_specs=P(("store", "rep"), None, "head"),
        check_vma=False,
    )
```

```python
import functools
import math

import jax
import jax.numpy as jnp
from jax import lax
from jax.experimental import pallas as pl
from jax.experimental.pallas import tpu as pltpu
from jax.sharding import PartitionSpec as P

HD = 128
BLK = 16
IDS = 8
FULL = 50 << 20
GROUP = 2
THETA = 1000000.0
SWAP = [(0, 1), (1, 0)]
ANY = pl.BlockSpec(memory_space=pl.ANY)
SMEM = pl.BlockSpec(memory_space=pltpu.SMEM)
VMEM = pl.BlockSpec(memory_space=pltpu.VMEM)
HBM = pl.BlockSpec(memory_space=pltpu.HBM)


def cost(flops, moved, trans=0):
    return pl.CostEstimate(flops=flops, bytes_accessed=moved, transcendentals=trans)


def angle_tables(positions):
    half = HD // 2
    lane = jnp.arange(HD, dtype=jnp.int32)
    inverse_freq = jnp.exp(
        -(2.0 * (lane % half).astype(jnp.float32) / HD) * math.log(THETA)
    )
    angles = positions.astype(jnp.float32)[..., None] * inverse_freq
    return jnp.cos(angles), jnp.where(lane < half, -1.0, 1.0) * jnp.sin(angles)


def turn(x, cosine, sine):
    x = x.astype(jnp.float32)
    other = jnp.concatenate([x[:, HD // 2 :], x[:, : HD // 2]], axis=1)
    return (x * cosine + other * sine).astype(jnp.bfloat16)


def pack_kernel(own_ref, other_ref, cache_ref, out_ref, held_ref, rows_ref, sems, out_sems):
    passages, kinds, page_len, _ = cache_ref.shape
    blocks = page_len // BLK
    rep = lax.axis_index("rep")
    lanes = pl.ds(pl.multiple_of(rep * HD, HD), HD)
    copies = [
        pltpu.make_async_copy(cache_ref.at[:, kind, :, lanes], held_ref.at[kind], sems.at[kind])
        for kind in range(kinds)
    ]
    for copy in copies:
        copy.start()
    row = lax.broadcasted_iota(jnp.int32, (IDS, HD), 0)
    lane = lax.broadcasted_iota(jnp.int32, (IDS, HD), 1)
    named = jnp.zeros((IDS, HD), jnp.int32)
    for slot in range(own_ref.shape[1]):
        named = jnp.where((row == rep) & (lane == slot), own_ref[0, slot], named)
        named = jnp.where((row == 1 - rep) & (lane == slot), other_ref[0, slot], named)
    named = named.astype(jnp.float32).astype(jnp.bfloat16)
    outs = []
    for kind in range(kinds):
        copies[kind].wait()
        for block in range(blocks):
            for passage in range(passages):
                rows_ref[kind * blocks + block, passage * BLK : (passage + 1) * BLK] = held_ref[
                    kind, passage, block * BLK : (block + 1) * BLK
                ]
            rows_ref[kind * blocks + block, passages * BLK :] = named
        part = pl.ds(kind * blocks, blocks)
        outs.append(
            pltpu.make_async_copy(rows_ref.at[part], out_ref.at[part], out_sems.at[kind])
        )
        outs[kind].start()
    for copy in outs:
        copy.wait()


def pack(own_ids, other_ids, page_cache):
    passages, kinds, page_len, _ = page_cache.shape
    shape = (kinds * page_len // BLK, passages * BLK + IDS, HD)
    return pl.pallas_call(
        pack_kernel,
        out_shape=jax.ShapeDtypeStruct(shape, jnp.bfloat16),
        in_specs=[SMEM, SMEM, HBM],
        out_specs=HBM,
        scratch_shapes=[
            pltpu.VMEM((kinds, passages, page_len, HD), jnp.bfloat16),
            pltpu.VMEM(shape, jnp.bfloat16),
            pltpu.SemaphoreType.DMA((kinds,)),
            pltpu.SemaphoreType.DMA((kinds,)),
        ],
        compiler_params=pltpu.CompilerParams(vmem_limit_bytes=FULL),
        cost_estimate=cost(0, 2 << 20),
        name="pack",
    )(own_ids, other_ids, page_cache)


def select_kernel(ids_ref, held_ref, out_ref, chosen_ref, sems):
    stores, requests, slots = out_ref.shape[:3]
    passages = (held_ref.shape[1] - IDS) // BLK
    shift = passages.bit_length() - 1
    assert passages == 1 << shift
    rep = lax.axis_index("rep")
    chunks = sems.shape[0]
    per = stores // chunks
    copies = []
    for chunk in range(chunks):

        def step(at, carry):
            dest = chunk * per + at
            for request in range(requests):
                row = dest * requests + (rep ^ request)
                for slot in range(slots):
                    wanted = ids_ref[row, slot]
                    start = pl.multiple_of((wanted & (passages - 1)) * BLK, BLK)
                    chosen_ref[dest, request, slot] = held_ref[
                        lax.shift_right_logical(wanted, shift), pl.ds(start, BLK)
                    ]
            return carry

        lax.fori_loop(0, per, step, 0, unroll=True)
        part = pl.ds(chunk * per, per)
        copy = pltpu.make_async_copy(chosen_ref.at[part], out_ref.at[part], sems.at[chunk])
        copy.start()
        copies.append(copy)
    for copy in copies:
        copy.wait()


def select(ids, held, stores):
    slots = ids.shape[1]
    requests = ids.shape[0] // stores
    shape = (stores, requests, slots, BLK, HD)
    return pl.pallas_call(
        select_kernel,
        out_shape=jax.ShapeDtypeStruct(shape, jnp.bfloat16),
        in_specs=[SMEM, VMEM],
        out_specs=HBM,
        scratch_shapes=[pltpu.VMEM(shape, jnp.bfloat16), pltpu.SemaphoreType.DMA((8,))],
        compiler_params=pltpu.CompilerParams(vmem_limit_bytes=8 << 20),
        cost_estimate=cost(0, 2 << 20),
        name="select",
    )(ids, held)


def split_kernel(q_ref, k_ref, v_ref, kept_ref, sent_ref):
    rep = lax.axis_index("rep")
    width = q_ref.shape[2] // 2
    for chosen in range(2):

        @pl.when(rep == chosen)
        def _():
            for part, out_ref in ((chosen, kept_ref), (1 - chosen, sent_ref)):
                out_ref[:, :width] = q_ref[0, :, part * width : (part + 1) * width]
                out_ref[:, width : width + HD] = k_ref[0, :, part * HD : (part + 1) * HD]
                out_ref[:, width + HD :] = v_ref[0, :, part * HD : (part + 1) * HD]


def split_heads(queries, span_keys, span_values):
    tokens = queries.shape[1]
    width = queries.shape[2] // 2 + 2 * HD
    shape = jax.ShapeDtypeStruct((tokens, width), jnp.bfloat16)
    return pl.pallas_call(
        split_kernel,
        out_shape=(shape, shape),
        in_specs=[VMEM] * 3,
        out_specs=(VMEM, VMEM),
        compiler_params=pltpu.CompilerParams(vmem_limit_bytes=8 << 20),
        cost_estimate=cost(0, 2 << 20),
        name="split_heads",
    )(queries, span_keys, span_values)


def rope_kernel(kept_ref, got_ref, cos_ref, sin_ref, out_ref):
    heads = out_ref.shape[1] - 1
    for request, x_ref in enumerate((kept_ref, got_ref)):
        for part in range(heads):
            out_ref[request, part] = turn(
                x_ref[:, part * HD : (part + 1) * HD], cos_ref[request], sin_ref[request]
            )
        out_ref[request, heads] = x_ref[:, heads * HD :]


def rope_heads(kept, got, cosine, sine):
    tokens, width = kept.shape
    return pl.pallas_call(
        rope_kernel,
        out_shape=jax.ShapeDtypeStruct((2, width // HD, tokens, HD), jnp.bfloat16),
        in_specs=[VMEM] * 4,
        out_specs=VMEM,
        compiler_params=pltpu.CompilerParams(vmem_limit_bytes=8 << 20),
        cost_estimate=cost(0, 2 << 20),
        name="rope_heads",
    )(kept, got, cosine, sine)


def attention_kernel(span_ref, far_ref, block_ref, token_ref, *refs, request):
    out_ref, key_ref = refs[-2:]
    heads = span_ref.shape[1] - 2
    tokens = span_ref.shape[2]
    far_len = key_ref.shape[0]
    blocks = far_ref.shape[0] // 2
    rows = GROUP * tokens
    shape = (GROUP, tokens, tokens)
    allowed = (
        lax.broadcasted_iota(jnp.int32, shape, 1) >= lax.broadcasted_iota(jnp.int32, shape, 2)
    ).reshape(rows, tokens)
    factor = math.log2(math.e) / math.sqrt(HD)
    contract = (((1,), (1,)), ((), ()))
    block_cos, block_sin = block_ref[0][:, None, :], block_ref[1][:, None, :]
    token_cos, token_sin = token_ref[0][None], token_ref[1][None]
    cosine = block_cos * token_cos - block_sin * token_sin
    sine = block_sin * token_cos + block_cos * token_sin
    key_ref[...] = turn(
        far_ref[:blocks, request].reshape(far_len, HD),
        cosine.reshape(far_len, HD),
        sine.reshape(far_len, HD),
    )

    def scores(first):
        q = span_ref[request, first : first + GROUP].reshape(rows, HD)
        far_s = lax.dot_general(q, key_ref[...], contract, preferred_element_type=jnp.float32)
        near_s = lax.dot_general(
            q, span_ref[request, heads], contract, preferred_element_type=jnp.float32
        )
        return far_s, jnp.where(allowed, near_s, -jnp.inf)

    def mix(first, far_s, near_s):
        row_max = jnp.maximum(
            jnp.max(far_s, axis=1, keepdims=True), jnp.max(near_s, axis=1, keepdims=True)
        )
        far_w = jnp.exp2((far_s - row_max) * factor)
        near_w = jnp.exp2((near_s - row_max) * factor)
        totals = jnp.sum(far_w, axis=1, keepdims=True) + jnp.sum(near_w, axis=1, keepdims=True)
        mixed = jnp.dot(
            far_w.astype(jnp.bfloat16),
            far_ref[blocks:, request].reshape(far_len, HD),
            preferred_element_type=jnp.float32,
        ) + jnp.dot(
            near_w.astype(jnp.bfloat16),
            span_ref[request, heads + 1],
            preferred_element_type=jnp.float32,
        )
        done = (mixed / totals).astype(jnp.bfloat16)
        for part in range(GROUP):
            out_ref[:, (first + part) * HD : (first + part + 1) * HD] = done[
                part * tokens : (part + 1) * tokens
            ]

    now = scores(0)
    for first in range(0, heads, GROUP):
        later = scores(first + GROUP) if first + GROUP < heads else None
        mix(first, *now)
        now = later


def attend(span, far, block_angles, token_angles, request, deps=()):
    _, parts, tokens, _ = span.shape
    heads = parts - 2
    far_len = block_angles.shape[1] * BLK
    return pl.pallas_call(
        functools.partial(attention_kernel, request=request),
        out_shape=jax.ShapeDtypeStruct((tokens, heads * HD), jnp.bfloat16),
        in_specs=[VMEM] * 4 + [HBM] * len(deps),
        out_specs=VMEM,
        scratch_shapes=[pltpu.VMEM((far_len, HD), jnp.bfloat16)],
        compiler_params=pltpu.CompilerParams(vmem_limit_bytes=FULL),
        cost_estimate=cost(
            4 * heads * tokens * (far_len + tokens) * HD,
            4 << 20,
            heads * tokens * (far_len + tokens),
        ),
        name=f"attend{request}",
    )(span, far, block_angles, token_angles, *deps)


def regroup_kernel(own_ref, other_ref, out_ref):
    for part, ref in enumerate((own_ref, other_ref)):
        out_ref[part] = jnp.swapaxes(ref[...], 0, 1)


def regroup(own, other):
    rows, blocks, cols = own.shape
    step = 256
    return pl.pallas_call(
        regroup_kernel,
        out_shape=jax.ShapeDtypeStruct((2, blocks, rows, cols), own.dtype),
        grid=(rows // step,),
        in_specs=[pl.BlockSpec((step, blocks, cols), lambda i: (i, 0, 0))] * 2,
        out_specs=pl.BlockSpec((2, blocks, step, cols), lambda i: (0, 0, i, 0)),
        compiler_params=pltpu.CompilerParams(vmem_limit_bytes=FULL),
        cost_estimate=cost(0, 32 << 20),
        name="regroup",
    )(own, other)


def project_kernel(own_ref, other_ref, w_ref, *refs, shifts, split):
    out_refs, (weight_ref, sems) = refs[:-2], refs[-2:]
    _, blocks, _, cols = w_ref.shape
    head, rep = lax.axis_index("head"), lax.axis_index("rep")
    copies = []
    for at, shift in enumerate(shifts):
        for part in range(2):
            copy = pltpu.make_async_copy(
                w_ref.at[part, lax.rem(head + shift, blocks)],
                weight_ref.at[at, part],
                sems.at[at, part],
            )
            copy.start()
            copies.append(copy)
    width = own_ref.shape[1]
    own_rows = pl.ds(pl.multiple_of(rep * width, width), width)
    other_rows = pl.ds(pl.multiple_of((1 - rep) * width, width), width)
    for at in range(len(shifts)):
        for part, place in enumerate((rep, 1 - rep)):
            copies[2 * at + part].wait()
            value = jnp.dot(
                own_ref[...], weight_ref[at, part, own_rows], preferred_element_type=jnp.float32
            ) + jnp.dot(
                other_ref[...],
                weight_ref[at, part, other_rows],
                preferred_element_type=jnp.float32,
            )
            lanes = pl.ds(pl.multiple_of(place * cols, cols), cols)
            if split:
                half = value.shape[0] // 2
                out_refs[0][:, lanes] = value[:half].astype(out_refs[0].dtype)
                out_refs[1][:, lanes] = value[half:].astype(out_refs[1].dtype)
            else:
                out_refs[at][:, lanes] = value


def project(own, other, weights, shifts, split=False):
    _, blocks, rows, cols = weights.shape
    tokens = own.shape[0]
    if split:
        shape = [jax.ShapeDtypeStruct((tokens // 2, 2 * cols), jnp.bfloat16)] * 2
    else:
        shape = [jax.ShapeDtypeStruct((tokens, 2 * cols), jnp.float32)] * len(shifts)
    return pl.pallas_call(
        functools.partial(project_kernel, shifts=shifts, split=split),
        out_shape=shape,
        in_specs=[VMEM, VMEM, HBM],
        out_specs=[VMEM] * len(shape),
        scratch_shapes=[
            pltpu.VMEM((len(shifts), 2, rows, cols), jnp.bfloat16),
            pltpu.SemaphoreType.DMA((len(shifts), 2)),
        ],
        compiler_params=pltpu.CompilerParams(vmem_limit_bytes=FULL),
        cost_estimate=cost(4 * tokens * rows * cols * len(shifts), len(shifts) * 4 << 20),
        name="project" + "".join(str(shift) for shift in shifts),
    )(own, other, weights)


def on_device(queries, span_keys, span_values, page_cache, passage_ids, starts, out_weight):
    stores = lax.axis_size("store")
    head_count = lax.axis_size("head")
    per_store, _, page_len, _ = page_cache.shape
    pass_count = passage_ids.shape[1]
    tokens = queries.shape[1]
    page_blocks = page_len // BLK

    other_ids = lax.ppermute(passage_ids, "rep", SWAP)
    held = lax.all_to_all(pack(passage_ids, other_ids, page_cache), "store", 0, 0, tiled=True)
    ids = held[:, per_store * BLK : per_store * BLK + 2, :pass_count].astype(jnp.int32)
    ids = ids.reshape(2 * stores, pass_count)

    out_weight, _ = lax.optimization_barrier((out_weight, other_ids))
    raw = out_weight[:, :, 0, :]
    weights = regroup(raw, lax.ppermute(raw, "rep", SWAP))
    kept, sent = split_heads(queries, span_keys, span_values)
    got = lax.ppermute(sent, "rep", SWAP)
    begins = jnp.concatenate([starts, lax.ppermute(starts, "rep", SWAP)])
    query_pos = (
        jnp.min(begins, axis=1, keepdims=True)
        + pass_count * page_len
        + jnp.arange(tokens, dtype=jnp.int32)
    )
    span = rope_heads(kept, got, *angle_tables(query_pos))
    block_pos = jnp.arange(page_blocks, dtype=jnp.int32)[None, :, None] * BLK + begins[:, None, :]
    block_angles = jnp.stack(angle_tables(block_pos.reshape(2, -1)), axis=1)
    token_angles = jnp.stack(angle_tables(jnp.arange(BLK, dtype=jnp.int32)))

    far = lax.all_to_all(select(ids, held, stores), "store", 0, 0, tiled=True)

    other = attend(span, far, block_angles[1], token_angles, 1, (weights,))
    other = lax.ppermute(other, "rep", SWAP)
    own = attend(span, far, block_angles[0], token_angles, 0)

    up = [(i, (i + 1) % head_count) for i in range(head_count)]
    down = [(i, (i - 1) % head_count) for i in range(head_count)]
    top, bottom = project(own, other, weights, (2,), split=True)
    top = lax.ppermute(top, "head", up).astype(jnp.float32)
    bottom = lax.ppermute(bottom, "head", down).astype(jnp.float32)
    above, below = project(own, other, weights, (1, 3))
    half = tokens // 2
    above = jnp.concatenate([above[:half] + top, above[half:]]).astype(jnp.bfloat16)
    below = jnp.concatenate([below[:half], below[half:] + bottom]).astype(jnp.bfloat16)
    above = lax.ppermute(above, "head", up).astype(jnp.float32)
    below = lax.ppermute(below, "head", down).astype(jnp.float32)
    (total,) = project(own, other, weights, (0,))
    return (total + above + below).astype(jnp.bfloat16)[None]


def solution(mesh):
    return jax.shard_map(
        on_device,
        mesh=mesh,
        in_specs=(
            P(("store", "rep"), None, "head"),
            P(("store", "rep"), None, "head"),
            P(("store", "rep"), None, "head"),
            P("store", None, None, "head"),
            P(("store", "rep"), None),
            P(("store", "rep"), None),
            P("head", None, "rep", None),
        ),
        out_specs=P(("store", "rep"), None, "head"),
        check_vma=False,
    )
```

```python
import functools
import math

import jax
import jax.numpy as jnp
from jax import lax
from jax.experimental import pallas as pl
from jax.experimental.pallas import tpu as pltpu
from jax.sharding import PartitionSpec as P

HD = 128
BLK = 16
IDS = 8
FULL = 24 << 20
GROUP = 2
THETA = 1000000.0
SWAP = [(0, 1), (1, 0)]
ANY = pl.BlockSpec(memory_space=pl.ANY)
SMEM = pl.BlockSpec(memory_space=pltpu.SMEM)
VMEM = pl.BlockSpec(memory_space=pltpu.VMEM)
HBM = pl.BlockSpec(memory_space=pltpu.HBM)


def in_hbm(x):
    return pltpu.with_memory_space_constraint(x, pltpu.HBM)


def cost(flops, moved, trans=0):
    return pl.CostEstimate(flops=flops, bytes_accessed=moved, transcendentals=trans)


def angle_tables(positions):
    half = HD // 2
    lane = jnp.arange(HD, dtype=jnp.int32)
    inverse_freq = jnp.exp(
        -(2.0 * (lane % half).astype(jnp.float32) / HD) * math.log(THETA)
    )
    angles = positions.astype(jnp.float32)[..., None] * inverse_freq
    return jnp.cos(angles), jnp.where(lane < half, -1.0, 1.0) * jnp.sin(angles)


def turn(x, cosine, sine):
    x = x.astype(jnp.float32)
    other = jnp.concatenate([x[:, HD // 2 :], x[:, : HD // 2]], axis=1)
    return (x * cosine + other * sine).astype(jnp.bfloat16)


def pack_kernel(own_ref, other_ref, cache_ref, out_ref, held_ref, rows_ref, sems, out_sems):
    passages, kinds, page_len, _ = cache_ref.shape
    blocks = page_len // BLK
    rep = lax.axis_index("rep")
    lanes = pl.ds(pl.multiple_of(rep * HD, HD), HD)
    copies = [
        pltpu.make_async_copy(cache_ref.at[:, kind, :, lanes], held_ref.at[kind], sems.at[kind])
        for kind in range(kinds)
    ]
    for copy in copies:
        copy.start()
    row = lax.broadcasted_iota(jnp.int32, (IDS, HD), 0)
    lane = lax.broadcasted_iota(jnp.int32, (IDS, HD), 1)
    named = jnp.zeros((IDS, HD), jnp.int32)
    for slot in range(own_ref.shape[1]):
        named = jnp.where((row == rep) & (lane == slot), own_ref[:, slot : slot + 1], named)
        named = jnp.where((row == 1 - rep) & (lane == slot), other_ref[:, slot : slot + 1], named)
    named = named.astype(jnp.float32).astype(jnp.bfloat16)
    outs = []
    for kind in range(kinds):
        copies[kind].wait()
        for block in range(blocks):
            for passage in range(passages):
                rows_ref[kind * blocks + block, passage * BLK : (passage + 1) * BLK] = held_ref[
                    kind, passage, block * BLK : (block + 1) * BLK
                ]
            rows_ref[kind * blocks + block, passages * BLK :] = named
        part = pl.ds(kind * blocks, blocks)
        outs.append(
            pltpu.make_async_copy(rows_ref.at[part], out_ref.at[part], out_sems.at[kind])
        )
        outs[kind].start()
    for copy in outs:
        copy.wait()


def pack(own_ids, other_ids, page_cache):
    passages, kinds, page_len, _ = page_cache.shape
    shape = (kinds * page_len // BLK, passages * BLK + IDS, HD)
    return pl.pallas_call(
        pack_kernel,
        out_shape=pltpu.HBM(shape, jnp.bfloat16),
        in_specs=[VMEM, VMEM, HBM],
        out_specs=HBM,
        scratch_shapes=[
            pltpu.VMEM((kinds, passages, page_len, HD), jnp.bfloat16),
            pltpu.VMEM(shape, jnp.bfloat16),
            pltpu.SemaphoreType.DMA((kinds,)),
            pltpu.SemaphoreType.DMA((kinds,)),
        ],
        compiler_params=pltpu.CompilerParams(vmem_limit_bytes=FULL),
        cost_estimate=cost(0, 2 << 20),
        name="pack",
    )(own_ids, other_ids, in_hbm(page_cache))


def select_kernel(ids_ref, held_ref, out_ref, chosen_ref, sems):
    stores, requests, slots = out_ref.shape[:3]
    passages = (held_ref.shape[1] - IDS) // BLK
    shift = passages.bit_length() - 1
    assert passages == 1 << shift
    rep = lax.axis_index("rep")
    chunks = sems.shape[0]
    per = stores // chunks

    def copy_out(chunk):
        part = pl.ds(chunk * per, per)
        return pltpu.make_async_copy(chosen_ref.at[part], out_ref.at[part], sems.at[chunk])

    def fill(chunk, carry):
        for at in range(per):
            dest = chunk * per + at
            for request in range(requests):
                row = dest * requests + (rep ^ request)
                for slot in range(slots):
                    wanted = ids_ref[row, slot]
                    start = pl.multiple_of((wanted & (passages - 1)) * BLK, BLK)
                    chosen_ref[dest, request, slot] = held_ref[
                        lax.shift_right_logical(wanted, shift), pl.ds(start, BLK)
                    ]
        copy_out(chunk).start()
        return carry

    lax.fori_loop(0, chunks, fill, 0)
    for chunk in range(chunks):
        copy_out(chunk).wait()


def select(ids, held, stores):
    slots = ids.shape[1]
    requests = ids.shape[0] // stores
    shape = (stores, requests, slots, BLK, HD)
    return pl.pallas_call(
        select_kernel,
        out_shape=pltpu.HBM(shape, jnp.bfloat16),
        in_specs=[SMEM, VMEM],
        out_specs=HBM,
        scratch_shapes=[pltpu.VMEM(shape, jnp.bfloat16), pltpu.SemaphoreType.DMA((8,))],
        compiler_params=pltpu.CompilerParams(vmem_limit_bytes=8 << 20),
        cost_estimate=cost(0, 2 << 20),
        name="select",
    )(ids, held)


def split_kernel(q_ref, k_ref, v_ref, kept_ref, sent_ref):
    rep = lax.axis_index("rep")
    width = q_ref.shape[2] // 2
    for chosen in range(2):

        @pl.when(rep == chosen)
        def _():
            for part, out_ref in ((chosen, kept_ref), (1 - chosen, sent_ref)):
                out_ref[:, :width] = q_ref[0, :, part * width : (part + 1) * width]
                out_ref[:, width : width + HD] = k_ref[0, :, part * HD : (part + 1) * HD]
                out_ref[:, width + HD :] = v_ref[0, :, part * HD : (part + 1) * HD]


def split_heads(queries, span_keys, span_values):
    tokens = queries.shape[1]
    width = queries.shape[2] // 2 + 2 * HD
    shape = jax.ShapeDtypeStruct((tokens, width), jnp.bfloat16)
    return pl.pallas_call(
        split_kernel,
        out_shape=(shape, shape),
        in_specs=[VMEM] * 3,
        out_specs=(VMEM, VMEM),
        compiler_params=pltpu.CompilerParams(vmem_limit_bytes=8 << 20),
        cost_estimate=cost(0, 2 << 20),
        name="split_heads",
    )(queries, span_keys, span_values)


def rope_kernel(kept_ref, got_ref, cos_ref, sin_ref, out_ref):
    heads = out_ref.shape[1] - 1
    for request, x_ref in enumerate((kept_ref, got_ref)):
        for part in range(heads):
            out_ref[request, part] = turn(
                x_ref[:, part * HD : (part + 1) * HD], cos_ref[request], sin_ref[request]
            )
        out_ref[request, heads] = x_ref[:, heads * HD :]


def rope_heads(kept, got, cosine, sine):
    tokens, width = kept.shape
    return pl.pallas_call(
        rope_kernel,
        out_shape=jax.ShapeDtypeStruct((2, width // HD, tokens, HD), jnp.bfloat16),
        in_specs=[VMEM] * 4,
        out_specs=VMEM,
        compiler_params=pltpu.CompilerParams(vmem_limit_bytes=8 << 20),
        cost_estimate=cost(0, 2 << 20),
        name="rope_heads",
    )(kept, got, cosine, sine)


def attention(span_ref, far_ref, block_ref, token_ref, out_ref, key_ref, request):
    heads = span_ref.shape[1] - 2
    tokens = span_ref.shape[2]
    far_len = key_ref.shape[0]
    blocks = far_ref.shape[0] // 2
    rows = GROUP * tokens
    shape = (GROUP, tokens, tokens)
    allowed = (
        lax.broadcasted_iota(jnp.int32, shape, 1) >= lax.broadcasted_iota(jnp.int32, shape, 2)
    ).reshape(rows, tokens)
    factor = math.log2(math.e) / math.sqrt(HD)
    contract = (((1,), (1,)), ((), ()))
    block_cos, block_sin = block_ref[0][:, None, :], block_ref[1][:, None, :]
    token_cos, token_sin = token_ref[0][None], token_ref[1][None]
    cosine = block_cos * token_cos - block_sin * token_sin
    sine = block_sin * token_cos + block_cos * token_sin
    key_ref[...] = turn(
        far_ref[:blocks, request].reshape(far_len, HD),
        cosine.reshape(far_len, HD),
        sine.reshape(far_len, HD),
    )

    def scores(first):
        q = span_ref[request, first : first + GROUP].reshape(rows, HD)
        far_s = lax.dot_general(q, key_ref[...], contract, preferred_element_type=jnp.float32)
        near_s = lax.dot_general(
            q, span_ref[request, heads], contract, preferred_element_type=jnp.float32
        )
        return far_s, jnp.where(allowed, near_s, -jnp.inf)

    def mix(first, far_s, near_s):
        row_max = jnp.maximum(
            jnp.max(far_s, axis=1, keepdims=True), jnp.max(near_s, axis=1, keepdims=True)
        )
        far_w = jnp.exp2((far_s - row_max) * factor)
        near_w = jnp.exp2((near_s - row_max) * factor)
        totals = jnp.sum(far_w, axis=1, keepdims=True) + jnp.sum(near_w, axis=1, keepdims=True)
        mixed = jnp.dot(
            far_w.astype(jnp.bfloat16),
            far_ref[blocks:, request].reshape(far_len, HD),
            preferred_element_type=jnp.float32,
        ) + jnp.dot(
            near_w.astype(jnp.bfloat16),
            span_ref[request, heads + 1],
            preferred_element_type=jnp.float32,
        )
        done = (mixed / totals).astype(jnp.bfloat16)
        for part in range(GROUP):
            out_ref[:, (first + part) * HD : (first + part + 1) * HD] = done[
                part * tokens : (part + 1) * tokens
            ]

    now = scores(0)
    for first in range(0, heads, GROUP):
        later = scores(first + GROUP) if first + GROUP < heads else None
        mix(first, *now)
        now = later


def fetch_weights(w_ref, out_refs, sems, shifts):
    blocks = w_ref.shape[1]
    rep, head = lax.axis_index("rep"), lax.axis_index("head")
    copies = []
    for at, (out_ref, shift) in enumerate(zip(out_refs, shifts)):
        width = out_ref.shape[2]
        block = lax.rem(head + jnp.where(rep == 0, shift[0], shift[1]), blocks)
        for part in range(2):
            for side, half in enumerate((rep, 1 - rep)):
                copy = pltpu.make_async_copy(
                    w_ref.at[part, block, pl.ds(pl.multiple_of(half * width, width), width)],
                    out_ref.at[part, side],
                    sems.at[at, part, side],
                )
                copy.start()
                copies.append(copy)
    return copies


def attention_kernel(span_ref, far_ref, block_ref, token_ref, w_ref, *refs, request, shifts):
    out_ref, *weight_refs, key_ref, sems = refs
    copies = fetch_weights(w_ref, weight_refs, sems, shifts)

    @pl.when(lax.axis_index("rep") >= 0)
    def _():
        attention(span_ref, far_ref, block_ref, token_ref, out_ref, key_ref, request)

    for copy in copies:
        copy.wait()


def attend(span, far, block_angles, token_angles, weights, request, shifts):
    _, parts, tokens, _ = span.shape
    heads = parts - 2
    far_len = block_angles.shape[1] * BLK
    _, _, rows, cols = weights.shape
    return pl.pallas_call(
        functools.partial(attention_kernel, request=request, shifts=shifts),
        out_shape=[jax.ShapeDtypeStruct((tokens, heads * HD), jnp.bfloat16)]
        + [pltpu.VMEM((2, 2, rows // 2, cols), weights.dtype)] * len(shifts),
        in_specs=[VMEM] * 4 + [HBM],
        out_specs=[VMEM] * (1 + len(shifts)),
        scratch_shapes=[
            pltpu.VMEM((far_len, HD), jnp.bfloat16),
            pltpu.SemaphoreType.DMA((len(shifts), 2, 2)),
        ],
        compiler_params=pltpu.CompilerParams(vmem_limit_bytes=FULL),
        cost_estimate=cost(
            4 * heads * tokens * (far_len + tokens) * HD,
            12 << 20,
            heads * tokens * (far_len + tokens),
        ),
        name=f"attend{request}",
    )(span, far, block_angles, token_angles, in_hbm(weights))


def regroup_kernel(own_ref, other_ref, out_ref):
    for part, ref in enumerate((own_ref, other_ref)):
        out_ref[part] = jnp.swapaxes(ref[...], 0, 1)


def regroup(own, other):
    rows, blocks, cols = own.shape
    step = 256
    return pl.pallas_call(
        regroup_kernel,
        out_shape=jax.ShapeDtypeStruct((2, blocks, rows, cols), own.dtype),
        grid=(rows // step,),
        in_specs=[pl.BlockSpec((step, blocks, cols), lambda i: (i, 0, 0))] * 2,
        out_specs=pl.BlockSpec((2, blocks, step, cols), lambda i: (0, 0, i, 0)),
        compiler_params=pltpu.CompilerParams(vmem_limit_bytes=FULL),
        cost_estimate=cost(0, 32 << 20),
        name="regroup",
    )(own, other)


def project_kernel(own_ref, other_ref, weight_ref, *refs):
    *more_refs, out_ref = refs
    rep = lax.axis_index("rep")
    cols = weight_ref.shape[3]
    for part, place in enumerate((rep, 1 - rep)):
        lanes = pl.ds(pl.multiple_of(place * cols, cols), cols)
        value = jnp.dot(
            own_ref[...], weight_ref[part, 0], preferred_element_type=jnp.float32
        ) + jnp.dot(other_ref[...], weight_ref[part, 1], preferred_element_type=jnp.float32)
        for more_ref in more_refs:
            value = value + more_ref[:, lanes].astype(jnp.float32)
        out_ref[:, lanes] = value.astype(out_ref.dtype)


def project(own, other, weight, dtype, name, *more):
    _, _, rows, cols = weight.shape
    tokens = own.shape[0]
    return pl.pallas_call(
        project_kernel,
        out_shape=jax.ShapeDtypeStruct((tokens, 2 * cols), dtype),
        in_specs=[VMEM] * (3 + len(more)),
        out_specs=VMEM,
        compiler_params=pltpu.CompilerParams(vmem_limit_bytes=FULL),
        cost_estimate=cost(8 * tokens * rows * cols, 4 << 20),
        name=name,
    )(own, other, weight, *more)


def on_device(queries, span_keys, span_values, page_cache, passage_ids, starts, out_weight):
    stores = lax.axis_size("store")
    head_count = lax.axis_size("head")
    per_store, _, page_len, _ = page_cache.shape
    pass_count = passage_ids.shape[1]
    tokens = queries.shape[1]
    page_blocks = page_len // BLK

    other_ids = lax.ppermute(passage_ids, "rep", SWAP)
    held = lax.all_to_all(pack(passage_ids, other_ids, page_cache), "store", 0, 0, tiled=True)
    ids = held[:, per_store * BLK : per_store * BLK + 2, :pass_count].astype(jnp.int32)
    ids = ids.reshape(2 * stores, pass_count)

    out_weight, _ = lax.optimization_barrier((out_weight, other_ids))
    raw = out_weight[:, :, 0, :]
    weights = regroup(raw, lax.ppermute(raw, "rep", SWAP))
    kept, sent = split_heads(queries, span_keys, span_values)
    got = lax.ppermute(sent, "rep", SWAP)
    begins = jnp.concatenate([starts, lax.ppermute(starts, "rep", SWAP)])
    query_pos = (
        jnp.min(begins, axis=1, keepdims=True)
        + pass_count * page_len
        + jnp.arange(tokens, dtype=jnp.int32)
    )
    span = rope_heads(kept, got, *angle_tables(query_pos))
    block_pos = jnp.arange(page_blocks, dtype=jnp.int32)[None, :, None] * BLK + begins[:, None, :]
    block_angles = jnp.stack(angle_tables(block_pos.reshape(2, -1)), axis=1)
    token_angles = jnp.stack(angle_tables(jnp.arange(BLK, dtype=jnp.int32)))

    far = lax.all_to_all(select(ids, held, stores), "store", 0, 0, tiled=True)

    other, opposite_w, plain_w = attend(
        span, far, block_angles[1], token_angles, weights, 1, ((2, 2), (3, 1))
    )
    other = lax.ppermute(other, "rep", SWAP)
    own, relayed_w, own_w = attend(
        span, far, block_angles[0], token_angles, weights, 0, ((1, 3), (0, 0))
    )

    ahead, behind = [], []
    for i in range(head_count):
        after, before = (i + 1) % head_count, (i - 1) % head_count
        ahead += [(2 * i, 2 * after), (2 * i + 1, 2 * before + 1)]
        behind += [(2 * i, 2 * before), (2 * i + 1, 2 * after + 1)]
    axes = ("head", "rep")
    opposite = project(own, other, opposite_w, jnp.bfloat16, "opposite")
    passing = lax.ppermute(opposite, axes, ahead)
    plain = project(own, other, plain_w, jnp.bfloat16, "plain")
    plain = lax.ppermute(plain, axes, behind)
    relayed = project(own, other, relayed_w, jnp.bfloat16, "relayed", passing)
    relayed = lax.ppermute(relayed, axes, ahead)
    total = project(own, other, own_w, jnp.float32, "kept")
    total = total + plain.astype(jnp.float32) + relayed.astype(jnp.float32)
    return total.astype(jnp.bfloat16)[None]


def solution(mesh):
    return jax.shard_map(
        on_device,
        mesh=mesh,
        in_specs=(
            P(("store", "rep"), None, "head"),
            P(("store", "rep"), None, "head"),
            P(("store", "rep"), None, "head"),
            P("store", None, None, "head"),
            P(("store", "rep"), None),
            P(("store", "rep"), None),
            P("head", None, "rep", None),
        ),
        out_specs=P(("store", "rep"), None, "head"),
        check_vma=False,
    )
```

```python
import functools
import math

import jax
import jax.numpy as jnp
from jax import lax
from jax.experimental import pallas as pl
from jax.experimental.pallas import tpu as pltpu
from jax.sharding import PartitionSpec as P

HD = 128
BLK = 16
IDS = 8
FULL = 24 << 20
GROUP = 2
THETA = 1000000.0
SWAP = [(0, 1), (1, 0)]
ANY = pl.BlockSpec(memory_space=pl.ANY)
SMEM = pl.BlockSpec(memory_space=pltpu.SMEM)
VMEM = pl.BlockSpec(memory_space=pltpu.VMEM)
HBM = pl.BlockSpec(memory_space=pltpu.HBM)


def in_hbm(x):
    return pltpu.with_memory_space_constraint(x, pltpu.HBM)


def cost(flops, moved, trans=0):
    return pl.CostEstimate(flops=flops, bytes_accessed=moved, transcendentals=trans)


def angle_tables(positions):
    half = HD // 2
    lane = jnp.arange(HD, dtype=jnp.int32)
    inverse_freq = jnp.exp(
        -(2.0 * (lane % half).astype(jnp.float32) / HD) * math.log(THETA)
    )
    angles = positions.astype(jnp.float32)[..., None] * inverse_freq
    return jnp.cos(angles), jnp.where(lane < half, -1.0, 1.0) * jnp.sin(angles)


def turn(x, cosine, sine):
    x = x.astype(jnp.float32)
    other = jnp.concatenate([x[:, HD // 2 :], x[:, : HD // 2]], axis=1)
    return (x * cosine + other * sine).astype(jnp.bfloat16)


def pack_kernel(cache_ref, out_ref, held_ref, rows_ref, sems, out_sems):
    passages, kinds, page_len, _ = cache_ref.shape
    blocks = page_len // BLK
    lanes = pl.ds(pl.multiple_of(lax.axis_index("rep") * HD, HD), HD)
    copies = [
        pltpu.make_async_copy(cache_ref.at[:, kind, :, lanes], held_ref.at[kind], sems.at[kind])
        for kind in range(kinds)
    ]
    for copy in copies:
        copy.start()
    outs = []
    for kind in range(kinds):
        copies[kind].wait()
        for block in range(blocks):
            for passage in range(passages):
                rows_ref[kind * blocks + block, passage * BLK : (passage + 1) * BLK] = held_ref[
                    kind, passage, block * BLK : (block + 1) * BLK
                ]
            rows_ref[kind * blocks + block, passages * BLK :] = jnp.zeros((IDS, HD), jnp.bfloat16)
        part = pl.ds(kind * blocks, blocks)
        outs.append(
            pltpu.make_async_copy(rows_ref.at[part], out_ref.at[part], out_sems.at[kind])
        )
        outs[kind].start()
    for copy in outs:
        copy.wait()


def pack(page_cache):
    passages, kinds, page_len, _ = page_cache.shape
    shape = (kinds * page_len // BLK, passages * BLK + IDS, HD)
    return pl.pallas_call(
        pack_kernel,
        out_shape=pltpu.HBM(shape, jnp.bfloat16),
        in_specs=[HBM],
        out_specs=HBM,
        scratch_shapes=[
            pltpu.VMEM((kinds, passages, page_len, HD), jnp.bfloat16),
            pltpu.VMEM(shape, jnp.bfloat16),
            pltpu.SemaphoreType.DMA((kinds,)),
            pltpu.SemaphoreType.DMA((kinds,)),
        ],
        compiler_params=pltpu.CompilerParams(vmem_limit_bytes=FULL),
        cost_estimate=cost(0, 2 << 20),
        name="pack",
    )(in_hbm(page_cache))


def select_kernel(first_ref, held_ref, out_ref, chosen_ref, sems):
    dests, slots, pieces = out_ref.shape[:3]
    chunks = sems.shape[0]
    per = dests // chunks

    def copy_out(chunk):
        part = pl.ds(chunk * per, per)
        return pltpu.make_async_copy(chosen_ref.at[part], out_ref.at[part], sems.at[chunk])

    def fill(chunk, carry):
        for at in range(per):
            dest = chunk * per + at
            for slot in range(slots):
                chosen_ref[dest, slot] = held_ref[pl.ds(first_ref[dest, slot], pieces)]
        copy_out(chunk).start()
        return carry

    lax.fori_loop(0, chunks, fill, 0)
    for chunk in range(chunks):
        copy_out(chunk).wait()


def select(first, held, pieces):
    shape = first.shape + (pieces,) + held.shape[1:]
    return pl.pallas_call(
        select_kernel,
        out_shape=pltpu.HBM(shape, jnp.bfloat16),
        in_specs=[SMEM, VMEM],
        out_specs=HBM,
        scratch_shapes=[pltpu.VMEM(shape, jnp.bfloat16), pltpu.SemaphoreType.DMA((8,))],
        compiler_params=pltpu.CompilerParams(vmem_limit_bytes=12 << 20),
        cost_estimate=cost(0, 2 << 20),
        name="select",
    )(first, held)


def split_kernel(q_ref, k_ref, v_ref, kept_ref, sent_ref):
    rep = lax.axis_index("rep")
    width = q_ref.shape[2] // 2
    for chosen in range(2):

        @pl.when(rep == chosen)
        def _():
            for part, out_ref in ((chosen, kept_ref), (1 - chosen, sent_ref)):
                out_ref[:, :width] = q_ref[0, :, part * width : (part + 1) * width]
                out_ref[:, width : width + HD] = k_ref[0, :, part * HD : (part + 1) * HD]
                out_ref[:, width + HD :] = v_ref[0, :, part * HD : (part + 1) * HD]


def split_heads(queries, span_keys, span_values):
    tokens = queries.shape[1]
    width = queries.shape[2] // 2 + 2 * HD
    shape = jax.ShapeDtypeStruct((tokens, width), jnp.bfloat16)
    return pl.pallas_call(
        split_kernel,
        out_shape=(shape, shape),
        in_specs=[VMEM] * 3,
        out_specs=(VMEM, VMEM),
        compiler_params=pltpu.CompilerParams(vmem_limit_bytes=8 << 20),
        cost_estimate=cost(0, 2 << 20),
        name="split_heads",
    )(queries, span_keys, span_values)


def rope_kernel(kept_ref, got_ref, cos_ref, sin_ref, out_ref):
    heads = out_ref.shape[1] - 1
    for request, x_ref in enumerate((kept_ref, got_ref)):
        for part in range(heads):
            out_ref[request, part] = turn(
                x_ref[:, part * HD : (part + 1) * HD], cos_ref[request], sin_ref[request]
            )
        out_ref[request, heads] = x_ref[:, heads * HD :]


def rope_heads(kept, got, cosine, sine):
    tokens, width = kept.shape
    return pl.pallas_call(
        rope_kernel,
        out_shape=jax.ShapeDtypeStruct((2, width // HD, tokens, HD), jnp.bfloat16),
        in_specs=[VMEM] * 4,
        out_specs=VMEM,
        compiler_params=pltpu.CompilerParams(vmem_limit_bytes=8 << 20),
        cost_estimate=cost(0, 2 << 20),
        name="rope_heads",
    )(kept, got, cosine, sine)


def attention(span_ref, far_ref, block_ref, token_ref, out_ref, key_ref, request):
    heads = span_ref.shape[1] - 2
    tokens = span_ref.shape[2]
    far_len = key_ref.shape[0]
    blocks = far_ref.shape[0] // 2
    rows = GROUP * tokens
    shape = (GROUP, tokens, tokens)
    allowed = (
        lax.broadcasted_iota(jnp.int32, shape, 1) >= lax.broadcasted_iota(jnp.int32, shape, 2)
    ).reshape(rows, tokens)
    factor = math.log2(math.e) / math.sqrt(HD)
    contract = (((1,), (1,)), ((), ()))
    block_cos, block_sin = block_ref[0][:, None, :], block_ref[1][:, None, :]
    token_cos, token_sin = token_ref[0][None], token_ref[1][None]
    cosine = block_cos * token_cos - block_sin * token_sin
    sine = block_sin * token_cos + block_cos * token_sin
    key_ref[...] = turn(
        far_ref[:blocks, request].reshape(far_len, HD),
        cosine.reshape(far_len, HD),
        sine.reshape(far_len, HD),
    )

    def scores(first):
        q = span_ref[request, first : first + GROUP].reshape(rows, HD)
        far_s = lax.dot_general(q, key_ref[...], contract, preferred_element_type=jnp.float32)
        near_s = lax.dot_general(
            q, span_ref[request, heads], contract, preferred_element_type=jnp.float32
        )
        return far_s, jnp.where(allowed, near_s, -jnp.inf)

    def mix(first, far_s, near_s):
        row_max = jnp.maximum(
            jnp.max(far_s, axis=1, keepdims=True), jnp.max(near_s, axis=1, keepdims=True)
        )
        far_w = jnp.exp2((far_s - row_max) * factor)
        near_w = jnp.exp2((near_s - row_max) * factor)
        totals = jnp.sum(far_w, axis=1, keepdims=True) + jnp.sum(near_w, axis=1, keepdims=True)
        mixed = jnp.dot(
            far_w.astype(jnp.bfloat16),
            far_ref[blocks:, request].reshape(far_len, HD),
            preferred_element_type=jnp.float32,
        ) + jnp.dot(
            near_w.astype(jnp.bfloat16),
            span_ref[request, heads + 1],
            preferred_element_type=jnp.float32,
        )
        done = (mixed / totals).astype(jnp.bfloat16)
        for part in range(GROUP):
            out_ref[:, (first + part) * HD : (first + part + 1) * HD] = done[
                part * tokens : (part + 1) * tokens
            ]

    now = scores(0)
    for first in range(0, heads, GROUP):
        later = scores(first + GROUP) if first + GROUP < heads else None
        mix(first, *now)
        now = later


def fetch_weights(w_ref, out_refs, sems, shifts):
    blocks = w_ref.shape[1]
    rep, head = lax.axis_index("rep"), lax.axis_index("head")
    copies = []
    for at, (out_ref, shift) in enumerate(zip(out_refs, shifts)):
        width = out_ref.shape[2]
        block = lax.rem(head + jnp.where(rep == 0, shift[0], shift[1]), blocks)
        for part in range(2):
            for side, half in enumerate((rep, 1 - rep)):
                copy = pltpu.make_async_copy(
                    w_ref.at[part, block, pl.ds(pl.multiple_of(half * width, width), width)],
                    out_ref.at[part, side],
                    sems.at[at, part, side],
                )
                copy.start()
                copies.append(copy)
    return copies


def attention_kernel(span_ref, far_ref, block_ref, token_ref, w_ref, *refs, request, shifts):
    out_ref, *weight_refs, key_ref, sems = refs
    copies = fetch_weights(w_ref, weight_refs, sems, shifts)

    @pl.when(lax.axis_index("rep") >= 0)
    def _():
        attention(span_ref, far_ref, block_ref, token_ref, out_ref, key_ref, request)

    for copy in copies:
        copy.wait()


def attend(span, far, block_angles, token_angles, weights, request, shifts):
    _, parts, tokens, _ = span.shape
    heads = parts - 2
    far_len = block_angles.shape[1] * BLK
    _, _, rows, cols = weights.shape
    return pl.pallas_call(
        functools.partial(attention_kernel, request=request, shifts=shifts),
        out_shape=[jax.ShapeDtypeStruct((tokens, heads * HD), jnp.bfloat16)]
        + [pltpu.VMEM((2, 2, rows // 2, cols), weights.dtype)] * len(shifts),
        in_specs=[VMEM] * 4 + [HBM],
        out_specs=[VMEM] * (1 + len(shifts)),
        scratch_shapes=[
            pltpu.VMEM((far_len, HD), jnp.bfloat16),
            pltpu.SemaphoreType.DMA((len(shifts), 2, 2)),
        ],
        compiler_params=pltpu.CompilerParams(vmem_limit_bytes=FULL),
        cost_estimate=cost(
            4 * heads * tokens * (far_len + tokens) * HD,
            12 << 20,
            heads * tokens * (far_len + tokens),
        ),
        name=f"attend{request}",
    )(span, far, block_angles, token_angles, in_hbm(weights))


def regroup_kernel(own_ref, other_ref, out_ref):
    for part, ref in enumerate((own_ref, other_ref)):
        out_ref[part] = jnp.swapaxes(ref[...], 0, 1)


def regroup(own, other):
    rows, blocks, cols = own.shape
    step = 256
    return pl.pallas_call(
        regroup_kernel,
        out_shape=jax.ShapeDtypeStruct((2, blocks, rows, cols), own.dtype),
        grid=(rows // step,),
        in_specs=[pl.BlockSpec((step, blocks, cols), lambda i: (i, 0, 0))] * 2,
        out_specs=pl.BlockSpec((2, blocks, step, cols), lambda i: (0, 0, i, 0)),
        compiler_params=pltpu.CompilerParams(vmem_limit_bytes=FULL),
        cost_estimate=cost(0, 32 << 20),
        name="regroup",
    )(own, other)


def project_kernel(own_ref, other_ref, weight_ref, *refs):
    *more_refs, out_ref = refs
    rep = lax.axis_index("rep")
    cols = weight_ref.shape[3]
    for part, place in enumerate((rep, 1 - rep)):
        lanes = pl.ds(pl.multiple_of(place * cols, cols), cols)
        value = jnp.dot(
            own_ref[...], weight_ref[part, 0], preferred_element_type=jnp.float32
        ) + jnp.dot(other_ref[...], weight_ref[part, 1], preferred_element_type=jnp.float32)
        for more_ref in more_refs:
            value = value + more_ref[:, lanes].astype(jnp.float32)
        out_ref[:, lanes] = value.astype(out_ref.dtype)


def project(own, other, weight, dtype, name, *more):
    _, _, rows, cols = weight.shape
    tokens = own.shape[0]
    return pl.pallas_call(
        project_kernel,
        out_shape=jax.ShapeDtypeStruct((tokens, 2 * cols), dtype),
        in_specs=[VMEM] * (3 + len(more)),
        out_specs=VMEM,
        compiler_params=pltpu.CompilerParams(vmem_limit_bytes=FULL),
        cost_estimate=cost(8 * tokens * rows * cols, 4 << 20),
        name=name,
    )(own, other, weight, *more)


def on_device(queries, span_keys, span_values, page_cache, passage_ids, starts, out_weight):
    stores = lax.axis_size("store")
    head_count = lax.axis_size("head")
    per_store, _, page_len, _ = page_cache.shape
    pass_count = passage_ids.shape[1]
    tokens = queries.shape[1]
    page_blocks = page_len // BLK

    rep = lax.axis_index("rep")
    other_ids = lax.ppermute(passage_ids, "rep", SWAP)
    row = jnp.arange(IDS, dtype=jnp.int32)[:, None]
    named = jnp.where(row == rep, passage_ids, jnp.where(row == 1 - rep, other_ids, 0))
    named = jnp.pad(named.astype(jnp.bfloat16), ((0, 0), (0, HD - pass_count)))
    packed = lax.dynamic_update_slice(
        pack(page_cache),
        jnp.broadcast_to(named, (stores, IDS, HD)),
        (0, per_store * BLK, 0),
    )
    held = lax.all_to_all(packed, "store", 0, 0, tiled=True)
    ids = held[:, per_store * BLK : per_store * BLK + 2, :pass_count].astype(jnp.int32)
    ids = jnp.where(rep == 0, ids, ids[:, ::-1]).reshape(2 * stores, pass_count)
    pieces = BLK // IDS
    first = ids // per_store * (per_store * pieces + 1) + ids % per_store * pieces
    chosen = select(first, held.reshape(-1, IDS, HD), pieces)
    chosen = chosen.reshape(stores, 2, pass_count, BLK, HD)

    out_weight, _ = lax.optimization_barrier((out_weight, packed))
    raw = out_weight[:, :, 0, :]
    weights = regroup(raw, lax.ppermute(raw, "rep", SWAP))
    kept, sent = split_heads(queries, span_keys, span_values)
    got = lax.ppermute(sent, "rep", SWAP)
    begins = jnp.concatenate([starts, lax.ppermute(starts, "rep", SWAP)])
    query_pos = (
        jnp.min(begins, axis=1, keepdims=True)
        + pass_count * page_len
        + jnp.arange(tokens, dtype=jnp.int32)
    )
    span = rope_heads(kept, got, *angle_tables(query_pos))
    block_pos = jnp.arange(page_blocks, dtype=jnp.int32)[None, :, None] * BLK + begins[:, None, :]
    block_angles = jnp.stack(angle_tables(block_pos.reshape(2, -1)), axis=1)
    token_angles = jnp.stack(angle_tables(jnp.arange(BLK, dtype=jnp.int32)))

    far = lax.all_to_all(chosen, "store", 0, 0, tiled=True)

    other, opposite_w, plain_w = attend(
        span, far, block_angles[1], token_angles, weights, 1, ((2, 2), (3, 1))
    )
    other = lax.ppermute(other, "rep", SWAP)
    own, relayed_w, own_w = attend(
        span, far, block_angles[0], token_angles, weights, 0, ((1, 3), (0, 0))
    )

    ahead, behind = [], []
    for i in range(head_count):
        after, before = (i + 1) % head_count, (i - 1) % head_count
        ahead += [(2 * i, 2 * after), (2 * i + 1, 2 * before + 1)]
        behind += [(2 * i, 2 * before), (2 * i + 1, 2 * after + 1)]
    axes = ("head", "rep")
    opposite = project(own, other, opposite_w, jnp.bfloat16, "opposite")
    passing = lax.ppermute(opposite, axes, ahead)
    plain = project(own, other, plain_w, jnp.bfloat16, "plain")
    plain = lax.ppermute(plain, axes, behind)
    relayed = project(own, other, relayed_w, jnp.bfloat16, "relayed", passing)
    relayed = lax.ppermute(relayed, axes, ahead)
    total = project(own, other, own_w, jnp.float32, "kept")
    total = total + plain.astype(jnp.float32) + relayed.astype(jnp.float32)
    return total.astype(jnp.bfloat16)[None]


def solution(mesh):
    return jax.shard_map(
        on_device,
        mesh=mesh,
        in_specs=(
            P(("store", "rep"), None, "head"),
            P(("store", "rep"), None, "head"),
            P(("store", "rep"), None, "head"),
            P("store", None, None, "head"),
            P(("store", "rep"), None),
            P(("store", "rep"), None),
            P("head", None, "rep", None),
        ),
        out_specs=P(("store", "rep"), None, "head"),
        check_vma=False,
    )
```

```python
import functools
import math

import jax
import jax.numpy as jnp
from jax import lax
from jax.experimental import pallas as pl
from jax.experimental.pallas import tpu as pltpu
from jax.sharding import PartitionSpec as P

HD = 128
BLK = 16
IDS = 8
FULL = 24 << 20
GROUP = 2
THETA = 1000000.0
SWAP = [(0, 1), (1, 0)]
ANY = pl.BlockSpec(memory_space=pl.ANY)
SMEM = pl.BlockSpec(memory_space=pltpu.SMEM)
VMEM = pl.BlockSpec(memory_space=pltpu.VMEM)
HBM = pl.BlockSpec(memory_space=pltpu.HBM)


def in_hbm(x):
    return pltpu.with_memory_space_constraint(x, pltpu.HBM)


def cost(flops, moved, trans=0):
    return pl.CostEstimate(flops=flops, bytes_accessed=moved, transcendentals=trans)


def angle_tables(positions):
    half = HD // 2
    lane = jnp.arange(HD, dtype=jnp.int32)
    inverse_freq = jnp.exp(
        -(2.0 * (lane % half).astype(jnp.float32) / HD) * math.log(THETA)
    )
    angles = positions.astype(jnp.float32)[..., None] * inverse_freq
    return jnp.cos(angles), jnp.where(lane < half, -1.0, 1.0) * jnp.sin(angles)


def turn(x, cosine, sine):
    x = x.astype(jnp.float32)
    other = jnp.concatenate([x[:, HD // 2 :], x[:, : HD // 2]], axis=1)
    return (x * cosine + other * sine).astype(jnp.bfloat16)


def pack_kernel(cache_ref, early_ref, out_ref, held_ref, rows_ref, sems, out_sems):
    passages, kinds, page_len, _ = cache_ref.shape
    blocks = page_len // BLK
    lanes = pl.ds(pl.multiple_of(lax.axis_index("rep") * HD, HD), HD)
    copies = [
        pltpu.make_async_copy(cache_ref.at[:, kind, :, lanes], held_ref.at[kind], sems.at[kind])
        for kind in range(kinds)
    ]
    for copy in copies:
        copy.start()
    outs = []
    for kind in range(kinds):
        copies[kind].wait()
        for block in range(blocks):
            for passage in range(passages):
                rows_ref[kind * blocks + block, passage * BLK : (passage + 1) * BLK] = held_ref[
                    kind, passage, block * BLK : (block + 1) * BLK
                ]
            rows_ref[kind * blocks + block, passages * BLK :] = jnp.zeros((IDS, HD), jnp.bfloat16)
        part = pl.ds(kind * blocks, blocks)
        outs.append(
            pltpu.make_async_copy(rows_ref.at[part], out_ref.at[part], out_sems.at[kind])
        )
        outs[kind].start()
    for copy in outs:
        copy.wait()


def pack(page_cache, early):
    passages, kinds, page_len, _ = page_cache.shape
    shape = (kinds * page_len // BLK, passages * BLK + IDS, HD)
    return pl.pallas_call(
        pack_kernel,
        out_shape=pltpu.HBM(shape, jnp.bfloat16),
        in_specs=[HBM, HBM],
        out_specs=HBM,
        scratch_shapes=[
            pltpu.VMEM((kinds, passages, page_len, HD), jnp.bfloat16),
            pltpu.VMEM(shape, jnp.bfloat16),
            pltpu.SemaphoreType.DMA((kinds,)),
            pltpu.SemaphoreType.DMA((kinds,)),
        ],
        compiler_params=pltpu.CompilerParams(vmem_limit_bytes=FULL),
        cost_estimate=cost(0, 2 << 20),
        name="pack",
    )(in_hbm(page_cache), in_hbm(early))


def select_kernel(first_ref, held_ref, out_ref, chosen_ref, sems):
    dests, slots, pieces = out_ref.shape[:3]
    chunks = sems.shape[0]
    per = dests // chunks

    def copy_out(chunk):
        part = pl.ds(chunk * per, per)
        return pltpu.make_async_copy(chosen_ref.at[part], out_ref.at[part], sems.at[chunk])

    def fill(chunk, carry):
        for at in range(per):
            dest = chunk * per + at
            for slot in range(slots):
                chosen_ref[dest, slot] = held_ref[pl.ds(first_ref[dest, slot], pieces)]
        copy_out(chunk).start()
        return carry

    lax.fori_loop(0, chunks, fill, 0)
    for chunk in range(chunks):
        copy_out(chunk).wait()


def select(first, held, pieces):
    shape = first.shape + (pieces,) + held.shape[1:]
    return pl.pallas_call(
        select_kernel,
        out_shape=pltpu.HBM(shape, jnp.bfloat16),
        in_specs=[SMEM, VMEM],
        out_specs=HBM,
        scratch_shapes=[pltpu.VMEM(shape, jnp.bfloat16), pltpu.SemaphoreType.DMA((8,))],
        compiler_params=pltpu.CompilerParams(vmem_limit_bytes=12 << 20),
        cost_estimate=cost(0, 2 << 20),
        name="select",
    )(first, held)


def split_kernel(q_ref, k_ref, v_ref, kept_ref, sent_ref):
    rep = lax.axis_index("rep")
    width = q_ref.shape[2] // 2
    for chosen in range(2):

        @pl.when(rep == chosen)
        def _():
            for part, out_ref in ((chosen, kept_ref), (1 - chosen, sent_ref)):
                out_ref[:, :width] = q_ref[0, :, part * width : (part + 1) * width]
                out_ref[:, width : width + HD] = k_ref[0, :, part * HD : (part + 1) * HD]
                out_ref[:, width + HD :] = v_ref[0, :, part * HD : (part + 1) * HD]


def split_heads(queries, span_keys, span_values):
    tokens = queries.shape[1]
    width = queries.shape[2] // 2 + 2 * HD
    shape = jax.ShapeDtypeStruct((tokens, width), jnp.bfloat16)
    return pl.pallas_call(
        split_kernel,
        out_shape=(shape, shape),
        in_specs=[VMEM] * 3,
        out_specs=(VMEM, VMEM),
        compiler_params=pltpu.CompilerParams(vmem_limit_bytes=8 << 20),
        cost_estimate=cost(0, 2 << 20),
        name="split_heads",
    )(queries, span_keys, span_values)


def rope_kernel(kept_ref, got_ref, cos_ref, sin_ref, out_ref):
    heads = out_ref.shape[1] - 1
    for request, x_ref in enumerate((kept_ref, got_ref)):
        for part in range(heads):
            out_ref[request, part] = turn(
                x_ref[:, part * HD : (part + 1) * HD], cos_ref[request], sin_ref[request]
            )
        out_ref[request, heads] = x_ref[:, heads * HD :]


def rope_heads(kept, got, cosine, sine):
    tokens, width = kept.shape
    return pl.pallas_call(
        rope_kernel,
        out_shape=jax.ShapeDtypeStruct((2, width // HD, tokens, HD), jnp.bfloat16),
        in_specs=[VMEM] * 4,
        out_specs=VMEM,
        compiler_params=pltpu.CompilerParams(vmem_limit_bytes=8 << 20),
        cost_estimate=cost(0, 2 << 20),
        name="rope_heads",
    )(kept, got, cosine, sine)


def attention(span_ref, far_ref, block_ref, token_ref, out_ref, key_ref, request):
    heads = span_ref.shape[1] - 2
    tokens = span_ref.shape[2]
    far_len = key_ref.shape[0]
    blocks = far_ref.shape[0] // 2
    rows = GROUP * tokens
    shape = (GROUP, tokens, tokens)
    allowed = (
        lax.broadcasted_iota(jnp.int32, shape, 1) >= lax.broadcasted_iota(jnp.int32, shape, 2)
    ).reshape(rows, tokens)
    factor = math.log2(math.e) / math.sqrt(HD)
    contract = (((1,), (1,)), ((), ()))
    block_cos, block_sin = block_ref[0][:, None, :], block_ref[1][:, None, :]
    token_cos, token_sin = token_ref[0][None], token_ref[1][None]
    cosine = block_cos * token_cos - block_sin * token_sin
    sine = block_sin * token_cos + block_cos * token_sin
    key_ref[...] = turn(
        far_ref[:blocks, request].reshape(far_len, HD),
        cosine.reshape(far_len, HD),
        sine.reshape(far_len, HD),
    )

    def scores(first):
        q = span_ref[request, first : first + GROUP].reshape(rows, HD)
        far_s = lax.dot_general(q, key_ref[...], contract, preferred_element_type=jnp.float32)
        near_s = lax.dot_general(
            q, span_ref[request, heads], contract, preferred_element_type=jnp.float32
        )
        return far_s, jnp.where(allowed, near_s, -jnp.inf)

    def mix(first, far_s, near_s):
        row_max = jnp.maximum(
            jnp.max(far_s, axis=1, keepdims=True), jnp.max(near_s, axis=1, keepdims=True)
        )
        far_w = jnp.exp2((far_s - row_max) * factor)
        near_w = jnp.exp2((near_s - row_max) * factor)
        totals = jnp.sum(far_w, axis=1, keepdims=True) + jnp.sum(near_w, axis=1, keepdims=True)
        mixed = jnp.dot(
            far_w.astype(jnp.bfloat16),
            far_ref[blocks:, request].reshape(far_len, HD),
            preferred_element_type=jnp.float32,
        ) + jnp.dot(
            near_w.astype(jnp.bfloat16),
            span_ref[request, heads + 1],
            preferred_element_type=jnp.float32,
        )
        done = (mixed / totals).astype(jnp.bfloat16)
        for part in range(GROUP):
            out_ref[:, (first + part) * HD : (first + part + 1) * HD] = done[
                part * tokens : (part + 1) * tokens
            ]

    now = scores(0)
    for first in range(0, heads, GROUP):
        later = scores(first + GROUP) if first + GROUP < heads else None
        mix(first, *now)
        now = later


def fetch_weights(w_ref, out_refs, sems, shifts):
    blocks = w_ref.shape[1]
    rep, head = lax.axis_index("rep"), lax.axis_index("head")
    copies = []
    for at, (out_ref, shift) in enumerate(zip(out_refs, shifts)):
        width = out_ref.shape[2]
        block = lax.rem(head + jnp.where(rep == 0, shift[0], shift[1]), blocks)
        for part in range(2):
            for side, half in enumerate((rep, 1 - rep)):
                copy = pltpu.make_async_copy(
                    w_ref.at[part, block, pl.ds(pl.multiple_of(half * width, width), width)],
                    out_ref.at[part, side],
                    sems.at[at, part, side],
                )
                copy.start()
                copies.append(copy)
    return copies


def attention_kernel(span_ref, far_ref, block_ref, token_ref, w_ref, *refs, request, shifts):
    out_ref, *weight_refs, key_ref, sems = refs
    copies = fetch_weights(w_ref, weight_refs, sems, shifts)

    @pl.when(lax.axis_index("rep") >= 0)
    def _():
        attention(span_ref, far_ref, block_ref, token_ref, out_ref, key_ref, request)

    for copy in copies:
        copy.wait()


def attend(span, far, block_angles, token_angles, weights, request, shifts):
    _, parts, tokens, _ = span.shape
    heads = parts - 2
    far_len = block_angles.shape[1] * BLK
    _, _, rows, cols = weights.shape
    return pl.pallas_call(
        functools.partial(attention_kernel, request=request, shifts=shifts),
        out_shape=[jax.ShapeDtypeStruct((tokens, heads * HD), jnp.bfloat16)]
        + [pltpu.VMEM((2, 2, rows // 2, cols), weights.dtype)] * len(shifts),
        in_specs=[VMEM] * 4 + [HBM],
        out_specs=[VMEM] * (1 + len(shifts)),
        scratch_shapes=[
            pltpu.VMEM((far_len, HD), jnp.bfloat16),
            pltpu.SemaphoreType.DMA((len(shifts), 2, 2)),
        ],
        compiler_params=pltpu.CompilerParams(vmem_limit_bytes=FULL),
        cost_estimate=cost(
            4 * heads * tokens * (far_len + tokens) * HD,
            12 << 20,
            heads * tokens * (far_len + tokens),
        ),
        name=f"attend{request}",
    )(span, far, block_angles, token_angles, in_hbm(weights))


def regroup_part(raw_ref, out_ref, rows_ref, blocks_ref, sems, out_sems):
    slots, step = rows_ref.shape[:2]
    chunks = raw_ref.shape[0] // step

    def copy_in(chunk):
        part = pl.ds(pl.multiple_of(chunk * step, step), step)
        slot = chunk % slots
        return pltpu.make_async_copy(raw_ref.at[part], rows_ref.at[slot], sems.at[slot])

    def copy_out(chunk):
        part = pl.ds(pl.multiple_of(chunk * step, step), step)
        slot = chunk % slots
        return pltpu.make_async_copy(blocks_ref.at[slot], out_ref.at[:, part], out_sems.at[slot])

    for chunk in range(slots):
        copy_in(chunk).start()

    def move(chunk, carry):
        copy_in(chunk).wait()

        @pl.when(chunk >= slots)
        def _():
            copy_out(chunk - slots).wait()

        blocks_ref[chunk % slots] = jnp.swapaxes(rows_ref[chunk % slots], 0, 1)
        copy_out(chunk).start()

        @pl.when(chunk + slots < chunks)
        def _():
            copy_in(chunk + slots).start()

        return carry

    lax.fori_loop(0, chunks, move, 0)
    for chunk in range(chunks - slots, chunks):
        copy_out(chunk).wait()


def regroup_scratch(raw):
    rows, blocks, cols = raw.shape
    step, slots = rows // 8, 2
    return [
        pltpu.VMEM((slots, step, blocks, cols), raw.dtype),
        pltpu.VMEM((slots, blocks, step, cols), raw.dtype),
        pltpu.SemaphoreType.DMA((slots,)),
        pltpu.SemaphoreType.DMA((slots,)),
    ]


def regroup_early_kernel(own_ref, ids_ref, out_ref, *scratch):
    @pl.when(lax.axis_index("rep") == 1)
    def _():
        regroup_part(own_ref, out_ref.at[0], *scratch)


def regroup_early(own, ids):
    rows, blocks, cols = own.shape
    return pl.pallas_call(
        regroup_early_kernel,
        out_shape=pltpu.HBM((2, blocks, rows, cols), own.dtype),
        in_specs=[HBM, ANY],
        out_specs=HBM,
        scratch_shapes=regroup_scratch(own),
        compiler_params=pltpu.CompilerParams(vmem_limit_bytes=FULL),
        cost_estimate=cost(0, 16 << 20),
        name="regroup_early",
    )(in_hbm(own), ids)


def regroup_late_kernel(own_ref, other_ref, early_ref, out_ref, *scratch):
    @pl.when(lax.axis_index("rep") == 0)
    def _():
        regroup_part(own_ref, out_ref.at[0], *scratch)

    regroup_part(other_ref, out_ref.at[1], *scratch)


def regroup_late(own, other, early):
    return pl.pallas_call(
        regroup_late_kernel,
        out_shape=pltpu.HBM(early.shape, early.dtype),
        in_specs=[HBM] * 3,
        out_specs=HBM,
        input_output_aliases={2: 0},
        scratch_shapes=regroup_scratch(own),
        compiler_params=pltpu.CompilerParams(vmem_limit_bytes=FULL),
        cost_estimate=cost(0, 32 << 20),
        name="regroup_late",
    )(in_hbm(own), in_hbm(other), early)


def project_kernel(own_ref, other_ref, weight_ref, *refs):
    *more_refs, out_ref = refs
    rep = lax.axis_index("rep")
    cols = weight_ref.shape[3]
    for part, place in enumerate((rep, 1 - rep)):
        lanes = pl.ds(pl.multiple_of(place * cols, cols), cols)
        value = jnp.dot(
            own_ref[...], weight_ref[part, 0], preferred_element_type=jnp.float32
        ) + jnp.dot(other_ref[...], weight_ref[part, 1], preferred_element_type=jnp.float32)
        for more_ref in more_refs:
            value = value + more_ref[:, lanes].astype(jnp.float32)
        out_ref[:, lanes] = value.astype(out_ref.dtype)


def project(own, other, weight, dtype, name, *more):
    _, _, rows, cols = weight.shape
    tokens = own.shape[0]
    return pl.pallas_call(
        project_kernel,
        out_shape=jax.ShapeDtypeStruct((tokens, 2 * cols), dtype),
        in_specs=[VMEM] * (3 + len(more)),
        out_specs=VMEM,
        compiler_params=pltpu.CompilerParams(vmem_limit_bytes=FULL),
        cost_estimate=cost(8 * tokens * rows * cols, 4 << 20),
        name=name,
    )(own, other, weight, *more)


def on_device(queries, span_keys, span_values, page_cache, passage_ids, starts, out_weight):
    stores = lax.axis_size("store")
    head_count = lax.axis_size("head")
    per_store, _, page_len, _ = page_cache.shape
    pass_count = passage_ids.shape[1]
    tokens = queries.shape[1]
    page_blocks = page_len // BLK

    rep = lax.axis_index("rep")
    other_ids = lax.ppermute(passage_ids, "rep", SWAP)
    out_weight, _ = lax.optimization_barrier((out_weight, other_ids))
    raw = out_weight[:, :, 0, :]
    other_raw = lax.ppermute(raw, "rep", SWAP)
    early = regroup_early(raw, other_ids)
    row = jnp.arange(IDS, dtype=jnp.int32)[:, None]
    named = jnp.where(row == rep, passage_ids, jnp.where(row == 1 - rep, other_ids, 0))
    named = jnp.pad(named.astype(jnp.bfloat16), ((0, 0), (0, HD - pass_count)))
    packed = lax.dynamic_update_slice(
        pack(page_cache, early),
        jnp.broadcast_to(named, (stores, IDS, HD)),
        (0, per_store * BLK, 0),
    )
    held = lax.all_to_all(packed, "store", 0, 0, tiled=True)
    ids = held[:, per_store * BLK : per_store * BLK + 2, :pass_count].astype(jnp.int32)
    ids = jnp.where(rep == 0, ids, ids[:, ::-1]).reshape(2 * stores, pass_count)
    pieces = BLK // IDS
    first = ids // per_store * (per_store * pieces + 1) + ids % per_store * pieces
    chosen = select(first, held.reshape(-1, IDS, HD), pieces)
    chosen = chosen.reshape(stores, 2, pass_count, BLK, HD)

    weights = regroup_late(raw, other_raw, early)
    kept, sent = split_heads(queries, span_keys, span_values)
    got = lax.ppermute(sent, "rep", SWAP)
    begins = jnp.concatenate([starts, lax.ppermute(starts, "rep", SWAP)])
    query_pos = (
        jnp.min(begins, axis=1, keepdims=True)
        + pass_count * page_len
        + jnp.arange(tokens, dtype=jnp.int32)
    )
    span = rope_heads(kept, got, *angle_tables(query_pos))
    block_pos = jnp.arange(page_blocks, dtype=jnp.int32)[None, :, None] * BLK + begins[:, None, :]
    block_angles = jnp.stack(angle_tables(block_pos.reshape(2, -1)), axis=1)
    token_angles = jnp.stack(angle_tables(jnp.arange(BLK, dtype=jnp.int32)))

    far = lax.all_to_all(chosen, "store", 0, 0, tiled=True)

    other, opposite_w, plain_w = attend(
        span, far, block_angles[1], token_angles, weights, 1, ((2, 2), (3, 1))
    )
    other = lax.ppermute(other, "rep", SWAP)
    own, relayed_w, own_w = attend(
        span, far, block_angles[0], token_angles, weights, 0, ((1, 3), (0, 0))
    )

    ahead, behind = [], []
    for i in range(head_count):
        after, before = (i + 1) % head_count, (i - 1) % head_count
        ahead += [(2 * i, 2 * after), (2 * i + 1, 2 * before + 1)]
        behind += [(2 * i, 2 * before), (2 * i + 1, 2 * after + 1)]
    axes = ("head", "rep")
    opposite = project(own, other, opposite_w, jnp.bfloat16, "opposite")
    passing = lax.ppermute(opposite, axes, ahead)
    plain = project(own, other, plain_w, jnp.bfloat16, "plain")
    plain = lax.ppermute(plain, axes, behind)
    relayed = project(own, other, relayed_w, jnp.bfloat16, "relayed", passing)
    relayed = lax.ppermute(relayed, axes, ahead)
    total = project(own, other, own_w, jnp.float32, "kept")
    total = total + plain.astype(jnp.float32) + relayed.astype(jnp.float32)
    return total.astype(jnp.bfloat16)[None]


def solution(mesh):
    return jax.shard_map(
        on_device,
        mesh=mesh,
        in_specs=(
            P(("store", "rep"), None, "head"),
            P(("store", "rep"), None, "head"),
            P(("store", "rep"), None, "head"),
            P("store", None, None, "head"),
            P(("store", "rep"), None),
            P(("store", "rep"), None),
            P("head", None, "rep", None),
        ),
        out_specs=P(("store", "rep"), None, "head"),
        check_vma=False,
    )
```

```python
import functools
import math

import jax
import jax.numpy as jnp
from jax import lax
from jax.experimental import pallas as pl
from jax.experimental.pallas import tpu as pltpu
from jax.sharding import PartitionSpec as P

HD = 128
BLK = 16
IDS = 8
FULL = 24 << 20
GROUP = 2
THETA = 1000000.0
SWAP = [(0, 1), (1, 0)]
ANY = pl.BlockSpec(memory_space=pl.ANY)
SMEM = pl.BlockSpec(memory_space=pltpu.SMEM)
VMEM = pl.BlockSpec(memory_space=pltpu.VMEM)
HBM = pl.BlockSpec(memory_space=pltpu.HBM)


def in_hbm(x):
    return pltpu.with_memory_space_constraint(x, pltpu.HBM)


def cost(flops, moved, trans=0):
    return pl.CostEstimate(flops=flops, bytes_accessed=moved, transcendentals=trans)


def angle_tables(positions):
    half = HD // 2
    lane = jnp.arange(HD, dtype=jnp.int32)
    inverse_freq = jnp.exp(
        -(2.0 * (lane % half).astype(jnp.float32) / HD) * math.log(THETA)
    )
    angles = positions.astype(jnp.float32)[..., None] * inverse_freq
    return jnp.cos(angles), jnp.where(lane < half, -1.0, 1.0) * jnp.sin(angles)


def turn(x, cosine, sine):
    x = x.astype(jnp.float32)
    other = jnp.concatenate([x[:, HD // 2 :], x[:, : HD // 2]], axis=1)
    return (x * cosine + other * sine).astype(jnp.bfloat16)


def pack_kernel(
    cache_ref, own_ref, other_ref, early_ref, out_ref, held_ref, ids_ref, rows_ref, *all_sems
):
    sems, out_sems, ids_sem = all_sems
    passages, kinds, page_len, _ = cache_ref.shape
    blocks = page_len // BLK
    rep = lax.axis_index("rep")
    lanes = pl.ds(pl.multiple_of(rep * HD, HD), HD)
    ids_copy = pltpu.make_async_copy(own_ref, ids_ref, ids_sem.at[0])
    ids_copy.start()
    copies = [
        pltpu.make_async_copy(cache_ref.at[:, kind, :, lanes], held_ref.at[kind], sems.at[kind])
        for kind in range(kinds)
    ]
    for copy in copies:
        copy.start()
    ids_copy.wait()
    row = lax.broadcasted_iota(jnp.int32, (IDS, HD), 0)
    lane = lax.broadcasted_iota(jnp.int32, (IDS, HD), 1)
    named = jnp.zeros((IDS, HD), jnp.int32)
    for slot in range(own_ref.shape[1]):
        at = slice(slot, slot + 1)
        named = jnp.where((row == rep) & (lane == slot), ids_ref[:, at], named)
        named = jnp.where((row == 1 - rep) & (lane == slot), other_ref[:, at], named)
    named = named.astype(jnp.float32).astype(jnp.bfloat16)
    outs = []
    for kind in range(kinds):
        copies[kind].wait()
        for block in range(blocks):
            for passage in range(passages):
                rows_ref[kind * blocks + block, passage * BLK : (passage + 1) * BLK] = held_ref[
                    kind, passage, block * BLK : (block + 1) * BLK
                ]
            rows_ref[kind * blocks + block, passages * BLK :] = named
        part = pl.ds(kind * blocks, blocks)
        outs.append(
            pltpu.make_async_copy(rows_ref.at[part], out_ref.at[part], out_sems.at[kind])
        )
        outs[kind].start()
    for copy in outs:
        copy.wait()


def pack(page_cache, own_ids, other_ids, early):
    passages, kinds, page_len, _ = page_cache.shape
    shape = (kinds * page_len // BLK, passages * BLK + IDS, HD)
    return pl.pallas_call(
        pack_kernel,
        out_shape=pltpu.HBM(shape, jnp.bfloat16),
        in_specs=[HBM, HBM, VMEM, HBM],
        out_specs=HBM,
        scratch_shapes=[
            pltpu.VMEM((kinds, passages, page_len, HD), jnp.bfloat16),
            pltpu.VMEM(own_ids.shape, own_ids.dtype),
            pltpu.VMEM(shape, jnp.bfloat16),
            pltpu.SemaphoreType.DMA((kinds,)),
            pltpu.SemaphoreType.DMA((kinds,)),
            pltpu.SemaphoreType.DMA((1,)),
        ],
        compiler_params=pltpu.CompilerParams(vmem_limit_bytes=FULL),
        cost_estimate=cost(0, 2 << 20),
        name="pack",
    )(in_hbm(page_cache), in_hbm(own_ids), other_ids, in_hbm(early))


def select_kernel(first_ref, held_ref, out_ref, chosen_ref, sems):
    dests, slots, pieces = out_ref.shape[:3]
    chunks = sems.shape[0]
    per = dests // chunks

    def copy_out(chunk):
        part = pl.ds(chunk * per, per)
        return pltpu.make_async_copy(chosen_ref.at[part], out_ref.at[part], sems.at[chunk])

    def fill(chunk, carry):
        for at in range(per):
            dest = chunk * per + at
            for slot in range(slots):
                chosen_ref[dest, slot] = held_ref[pl.ds(first_ref[dest, slot], pieces)]
        copy_out(chunk).start()
        return carry

    lax.fori_loop(0, chunks, fill, 0)
    for chunk in range(chunks):
        copy_out(chunk).wait()


def select(first, held, pieces):
    shape = first.shape + (pieces,) + held.shape[1:]
    return pl.pallas_call(
        select_kernel,
        out_shape=pltpu.HBM(shape, jnp.bfloat16),
        in_specs=[SMEM, VMEM],
        out_specs=HBM,
        scratch_shapes=[pltpu.VMEM(shape, jnp.bfloat16), pltpu.SemaphoreType.DMA((8,))],
        compiler_params=pltpu.CompilerParams(vmem_limit_bytes=12 << 20),
        cost_estimate=cost(0, 2 << 20),
        name="select",
    )(first, held)


def split_kernel(q_ref, k_ref, v_ref, kept_ref, sent_ref):
    rep = lax.axis_index("rep")
    width = q_ref.shape[2] // 2
    for chosen in range(2):

        @pl.when(rep == chosen)
        def _():
            for part, out_ref in ((chosen, kept_ref), (1 - chosen, sent_ref)):
                out_ref[:, :width] = q_ref[0, :, part * width : (part + 1) * width]
                out_ref[:, width : width + HD] = k_ref[0, :, part * HD : (part + 1) * HD]
                out_ref[:, width + HD :] = v_ref[0, :, part * HD : (part + 1) * HD]


def split_heads(queries, span_keys, span_values):
    tokens = queries.shape[1]
    width = queries.shape[2] // 2 + 2 * HD
    shape = jax.ShapeDtypeStruct((tokens, width), jnp.bfloat16)
    return pl.pallas_call(
        split_kernel,
        out_shape=(shape, shape),
        in_specs=[VMEM] * 3,
        out_specs=(VMEM, VMEM),
        compiler_params=pltpu.CompilerParams(vmem_limit_bytes=8 << 20),
        cost_estimate=cost(0, 2 << 20),
        name="split_heads",
    )(queries, span_keys, span_values)


def rope_kernel(kept_ref, got_ref, cos_ref, sin_ref, out_ref):
    heads = out_ref.shape[1] - 1
    for request, x_ref in enumerate((kept_ref, got_ref)):
        for part in range(heads):
            out_ref[request, part] = turn(
                x_ref[:, part * HD : (part + 1) * HD], cos_ref[request], sin_ref[request]
            )
        out_ref[request, heads] = x_ref[:, heads * HD :]


def rope_heads(kept, got, cosine, sine):
    tokens, width = kept.shape
    return pl.pallas_call(
        rope_kernel,
        out_shape=jax.ShapeDtypeStruct((2, width // HD, tokens, HD), jnp.bfloat16),
        in_specs=[VMEM] * 4,
        out_specs=VMEM,
        compiler_params=pltpu.CompilerParams(vmem_limit_bytes=8 << 20),
        cost_estimate=cost(0, 2 << 20),
        name="rope_heads",
    )(kept, got, cosine, sine)


def attention(span_ref, far_ref, block_ref, token_ref, out_ref, key_ref, request):
    heads = span_ref.shape[1] - 2
    tokens = span_ref.shape[2]
    far_len = key_ref.shape[0]
    blocks = far_ref.shape[0] // 2
    rows = GROUP * tokens
    shape = (GROUP, tokens, tokens)
    allowed = (
        lax.broadcasted_iota(jnp.int32, shape, 1) >= lax.broadcasted_iota(jnp.int32, shape, 2)
    ).reshape(rows, tokens)
    factor = math.log2(math.e) / math.sqrt(HD)
    contract = (((1,), (1,)), ((), ()))
    block_cos, block_sin = block_ref[0][:, None, :], block_ref[1][:, None, :]
    token_cos, token_sin = token_ref[0][None], token_ref[1][None]
    cosine = block_cos * token_cos - block_sin * token_sin
    sine = block_sin * token_cos + block_cos * token_sin
    key_ref[...] = turn(
        far_ref[:blocks, request].reshape(far_len, HD),
        cosine.reshape(far_len, HD),
        sine.reshape(far_len, HD),
    )

    def scores(first):
        q = span_ref[request, first : first + GROUP].reshape(rows, HD)
        far_s = lax.dot_general(q, key_ref[...], contract, preferred_element_type=jnp.float32)
        near_s = lax.dot_general(
            q, span_ref[request, heads], contract, preferred_element_type=jnp.float32
        )
        return far_s, jnp.where(allowed, near_s, -jnp.inf)

    def mix(first, far_s, near_s):
        row_max = jnp.maximum(
            jnp.max(far_s, axis=1, keepdims=True), jnp.max(near_s, axis=1, keepdims=True)
        )
        far_w = jnp.exp2((far_s - row_max) * factor)
        near_w = jnp.exp2((near_s - row_max) * factor)
        totals = jnp.sum(far_w, axis=1, keepdims=True) + jnp.sum(near_w, axis=1, keepdims=True)
        mixed = jnp.dot(
            far_w.astype(jnp.bfloat16),
            far_ref[blocks:, request].reshape(far_len, HD),
            preferred_element_type=jnp.float32,
        ) + jnp.dot(
            near_w.astype(jnp.bfloat16),
            span_ref[request, heads + 1],
            preferred_element_type=jnp.float32,
        )
        done = (mixed / totals).astype(jnp.bfloat16)
        for part in range(GROUP):
            out_ref[:, (first + part) * HD : (first + part + 1) * HD] = done[
                part * tokens : (part + 1) * tokens
            ]

    now = scores(0)
    for first in range(0, heads, GROUP):
        later = scores(first + GROUP) if first + GROUP < heads else None
        mix(first, *now)
        now = later


def fetch_weights(w_ref, out_refs, sems, shifts):
    blocks = w_ref.shape[1]
    rep, head = lax.axis_index("rep"), lax.axis_index("head")
    copies = []
    for at, (out_ref, shift) in enumerate(zip(out_refs, shifts)):
        width = out_ref.shape[2]
        block = lax.rem(head + jnp.where(rep == 0, shift[0], shift[1]), blocks)
        for part in range(2):
            for side, half in enumerate((rep, 1 - rep)):
                copy = pltpu.make_async_copy(
                    w_ref.at[part, block, pl.ds(pl.multiple_of(half * width, width), width)],
                    out_ref.at[part, side],
                    sems.at[at, part, side],
                )
                copy.start()
                copies.append(copy)
    return copies


def attention_kernel(span_ref, far_ref, block_ref, token_ref, w_ref, *refs, request, shifts):
    out_ref, *weight_refs, key_ref, sems = refs
    copies = fetch_weights(w_ref, weight_refs, sems, shifts)

    @pl.when(lax.axis_index("rep") >= 0)
    def _():
        attention(span_ref, far_ref, block_ref, token_ref, out_ref, key_ref, request)

    for copy in copies:
        copy.wait()


def attend(span, far, block_angles, token_angles, weights, request, shifts):
    _, parts, tokens, _ = span.shape
    heads = parts - 2
    far_len = block_angles.shape[1] * BLK
    _, _, rows, cols = weights.shape
    return pl.pallas_call(
        functools.partial(attention_kernel, request=request, shifts=shifts),
        out_shape=[jax.ShapeDtypeStruct((tokens, heads * HD), jnp.bfloat16)]
        + [pltpu.VMEM((2, 2, rows // 2, cols), weights.dtype)] * len(shifts),
        in_specs=[VMEM] * 4 + [HBM],
        out_specs=[VMEM] * (1 + len(shifts)),
        scratch_shapes=[
            pltpu.VMEM((far_len, HD), jnp.bfloat16),
            pltpu.SemaphoreType.DMA((len(shifts), 2, 2)),
        ],
        compiler_params=pltpu.CompilerParams(vmem_limit_bytes=FULL),
        cost_estimate=cost(
            4 * heads * tokens * (far_len + tokens) * HD,
            12 << 20,
            heads * tokens * (far_len + tokens),
        ),
        name=f"attend{request}",
    )(span, far, block_angles, token_angles, in_hbm(weights))


def regroup_part(raw_ref, out_ref, rows_ref, blocks_ref, sems, out_sems):
    slots, step = rows_ref.shape[:2]
    chunks = raw_ref.shape[0] // step

    def copy_in(chunk):
        part = pl.ds(pl.multiple_of(chunk * step, step), step)
        slot = chunk % slots
        return pltpu.make_async_copy(raw_ref.at[part], rows_ref.at[slot], sems.at[slot])

    def copy_out(chunk):
        part = pl.ds(pl.multiple_of(chunk * step, step), step)
        slot = chunk % slots
        return pltpu.make_async_copy(blocks_ref.at[slot], out_ref.at[:, part], out_sems.at[slot])

    for chunk in range(slots):
        copy_in(chunk).start()

    def move(chunk, carry):
        copy_in(chunk).wait()

        @pl.when(chunk >= slots)
        def _():
            copy_out(chunk - slots).wait()

        blocks_ref[chunk % slots] = jnp.swapaxes(rows_ref[chunk % slots], 0, 1)
        copy_out(chunk).start()

        @pl.when(chunk + slots < chunks)
        def _():
            copy_in(chunk + slots).start()

        return carry

    lax.fori_loop(0, chunks, move, 0)
    for chunk in range(chunks - slots, chunks):
        copy_out(chunk).wait()


def regroup_scratch(raw):
    rows, blocks, cols = raw.shape
    step, slots = rows // 8, 2
    return [
        pltpu.VMEM((slots, step, blocks, cols), raw.dtype),
        pltpu.VMEM((slots, blocks, step, cols), raw.dtype),
        pltpu.SemaphoreType.DMA((slots,)),
        pltpu.SemaphoreType.DMA((slots,)),
    ]


def regroup_early_kernel(own_ref, ids_ref, out_ref, *scratch):
    @pl.when(lax.axis_index("rep") == 1)
    def _():
        regroup_part(own_ref, out_ref.at[0], *scratch)


def regroup_early(own, ids):
    rows, blocks, cols = own.shape
    return pl.pallas_call(
        regroup_early_kernel,
        out_shape=pltpu.HBM((2, blocks, rows, cols), own.dtype),
        in_specs=[HBM, ANY],
        out_specs=HBM,
        scratch_shapes=regroup_scratch(own),
        compiler_params=pltpu.CompilerParams(vmem_limit_bytes=FULL),
        cost_estimate=cost(0, 16 << 20),
        name="regroup_early",
    )(in_hbm(own), ids)


def regroup_late_kernel(own_ref, other_ref, early_ref, out_ref, *scratch):
    @pl.when(lax.axis_index("rep") == 0)
    def _():
        regroup_part(own_ref, out_ref.at[0], *scratch)

    regroup_part(other_ref, out_ref.at[1], *scratch)


def regroup_late(own, other, early):
    return pl.pallas_call(
        regroup_late_kernel,
        out_shape=pltpu.HBM(early.shape, early.dtype),
        in_specs=[HBM] * 3,
        out_specs=HBM,
        input_output_aliases={2: 0},
        scratch_shapes=regroup_scratch(own),
        compiler_params=pltpu.CompilerParams(vmem_limit_bytes=FULL),
        cost_estimate=cost(0, 32 << 20),
        name="regroup_late",
    )(in_hbm(own), in_hbm(other), early)


def project_kernel(own_ref, other_ref, weight_ref, *refs):
    *more_refs, out_ref = refs
    rep = lax.axis_index("rep")
    cols = weight_ref.shape[3]
    for part, place in enumerate((rep, 1 - rep)):
        lanes = pl.ds(pl.multiple_of(place * cols, cols), cols)
        value = jnp.dot(
            own_ref[...], weight_ref[part, 0], preferred_element_type=jnp.float32
        ) + jnp.dot(other_ref[...], weight_ref[part, 1], preferred_element_type=jnp.float32)
        for more_ref in more_refs:
            value = value + more_ref[:, lanes].astype(jnp.float32)
        out_ref[:, lanes] = value.astype(out_ref.dtype)


def project(own, other, weight, dtype, name, *more):
    _, _, rows, cols = weight.shape
    tokens = own.shape[0]
    return pl.pallas_call(
        project_kernel,
        out_shape=jax.ShapeDtypeStruct((tokens, 2 * cols), dtype),
        in_specs=[VMEM] * (3 + len(more)),
        out_specs=VMEM,
        compiler_params=pltpu.CompilerParams(vmem_limit_bytes=FULL),
        cost_estimate=cost(8 * tokens * rows * cols, 4 << 20),
        name=name,
    )(own, other, weight, *more)


def on_device(queries, span_keys, span_values, page_cache, passage_ids, starts, out_weight):
    stores = lax.axis_size("store")
    head_count = lax.axis_size("head")
    per_store, _, page_len, _ = page_cache.shape
    pass_count = passage_ids.shape[1]
    tokens = queries.shape[1]
    page_blocks = page_len // BLK

    rep = lax.axis_index("rep")
    other_ids = lax.ppermute(passage_ids, "rep", SWAP)
    out_weight, _ = lax.optimization_barrier((out_weight, other_ids))
    raw = out_weight[:, :, 0, :]
    other_raw = lax.ppermute(raw, "rep", SWAP)
    early = regroup_early(raw, other_ids)
    packed = pack(page_cache, passage_ids, other_ids, early)
    held = lax.all_to_all(packed, "store", 0, 0, tiled=True)
    ids = held[:, per_store * BLK : per_store * BLK + 2, :pass_count].astype(jnp.int32)
    ids = jnp.where(rep == 0, ids, ids[:, ::-1]).reshape(2 * stores, pass_count)
    pieces = BLK // IDS
    first = ids // per_store * (per_store * pieces + 1) + ids % per_store * pieces
    chosen = select(first, held.reshape(-1, IDS, HD), pieces)
    chosen = chosen.reshape(stores, 2, pass_count, BLK, HD)

    weights = regroup_late(raw, other_raw, early)
    kept, sent = split_heads(queries, span_keys, span_values)
    got = lax.ppermute(sent, "rep", SWAP)
    begins = jnp.concatenate([starts, lax.ppermute(starts, "rep", SWAP)])
    query_pos = (
        jnp.min(begins, axis=1, keepdims=True)
        + pass_count * page_len
        + jnp.arange(tokens, dtype=jnp.int32)
    )
    span = rope_heads(kept, got, *angle_tables(query_pos))
    block_pos = jnp.arange(page_blocks, dtype=jnp.int32)[None, :, None] * BLK + begins[:, None, :]
    block_angles = jnp.stack(angle_tables(block_pos.reshape(2, -1)), axis=1)
    token_angles = jnp.stack(angle_tables(jnp.arange(BLK, dtype=jnp.int32)))

    far = lax.all_to_all(chosen, "store", 0, 0, tiled=True)

    other, opposite_w, plain_w = attend(
        span, far, block_angles[1], token_angles, weights, 1, ((2, 2), (3, 1))
    )
    other = lax.ppermute(other, "rep", SWAP)
    own, relayed_w, own_w = attend(
        span, far, block_angles[0], token_angles, weights, 0, ((1, 3), (0, 0))
    )

    ahead, behind = [], []
    for i in range(head_count):
        after, before = (i + 1) % head_count, (i - 1) % head_count
        ahead += [(2 * i, 2 * after), (2 * i + 1, 2 * before + 1)]
        behind += [(2 * i, 2 * before), (2 * i + 1, 2 * after + 1)]
    axes = ("head", "rep")
    opposite = project(own, other, opposite_w, jnp.bfloat16, "opposite")
    passing = lax.ppermute(opposite, axes, ahead)
    plain = project(own, other, plain_w, jnp.bfloat16, "plain")
    plain = lax.ppermute(plain, axes, behind)
    relayed = project(own, other, relayed_w, jnp.bfloat16, "relayed", passing)
    relayed = lax.ppermute(relayed, axes, ahead)
    total = project(own, other, own_w, jnp.float32, "kept")
    total = total + plain.astype(jnp.float32) + relayed.astype(jnp.float32)
    return total.astype(jnp.bfloat16)[None]


def solution(mesh):
    return jax.shard_map(
        on_device,
        mesh=mesh,
        in_specs=(
            P(("store", "rep"), None, "head"),
            P(("store", "rep"), None, "head"),
            P(("store", "rep"), None, "head"),
            P("store", None, None, "head"),
            P(("store", "rep"), None),
            P(("store", "rep"), None),
            P("head", None, "rep", None),
        ),
        out_specs=P(("store", "rep"), None, "head"),
        check_vma=False,
    )
```

```python
import functools
import math

import jax
import jax.numpy as jnp
from jax import lax
from jax.experimental import pallas as pl
from jax.experimental.pallas import tpu as pltpu
from jax.sharding import PartitionSpec as P

HD = 128
BLK = 16
IDS = 8
FULL = 24 << 20
GROUP = 2
THETA = 1000000.0
SWAP = [(0, 1), (1, 0)]
ANY = pl.BlockSpec(memory_space=pl.ANY)
SMEM = pl.BlockSpec(memory_space=pltpu.SMEM)
VMEM = pl.BlockSpec(memory_space=pltpu.VMEM)
HBM = pl.BlockSpec(memory_space=pltpu.HBM)


def in_hbm(x):
    return pltpu.with_memory_space_constraint(x, pltpu.HBM)


def cost(flops, moved, trans=0):
    return pl.CostEstimate(flops=flops, bytes_accessed=moved, transcendentals=trans)


def angle_tables(positions):
    half = HD // 2
    lane = jnp.arange(HD, dtype=jnp.int32)
    inverse_freq = jnp.exp(
        -(2.0 * (lane % half).astype(jnp.float32) / HD) * math.log(THETA)
    )
    angles = positions.astype(jnp.float32)[..., None] * inverse_freq
    return jnp.cos(angles), jnp.where(lane < half, -1.0, 1.0) * jnp.sin(angles)


def turn(x, cosine, sine):
    x = x.astype(jnp.float32)
    other = jnp.concatenate([x[:, HD // 2 :], x[:, : HD // 2]], axis=1)
    return (x * cosine + other * sine).astype(jnp.bfloat16)


def pack_kernel(
    cache_ref, own_ref, other_ref, early_ref, out_ref, held_ref, ids_ref, rows_ref, *all_sems
):
    sems, out_sems, ids_sem = all_sems
    passages, kinds, page_len, _ = cache_ref.shape
    blocks = page_len // BLK
    rep = lax.axis_index("rep")
    lanes = pl.ds(pl.multiple_of(rep * HD, HD), HD)
    ids_copy = pltpu.make_async_copy(own_ref, ids_ref, ids_sem.at[0])
    ids_copy.start()
    copies = [
        pltpu.make_async_copy(cache_ref.at[:, kind, :, lanes], held_ref.at[kind], sems.at[kind])
        for kind in range(kinds)
    ]
    for copy in copies:
        copy.start()
    ids_copy.wait()
    row = lax.broadcasted_iota(jnp.int32, (IDS, HD), 0)
    lane = lax.broadcasted_iota(jnp.int32, (IDS, HD), 1)
    named = jnp.zeros((IDS, HD), jnp.int32)
    for slot in range(own_ref.shape[1]):
        at = slice(slot, slot + 1)
        named = jnp.where((row == rep) & (lane == slot), ids_ref[:, at], named)
        named = jnp.where((row == 1 - rep) & (lane == slot), other_ref[:, at], named)
    named = named.astype(jnp.float32).astype(jnp.bfloat16)
    outs = []
    for kind in range(kinds):
        copies[kind].wait()
        for block in range(blocks):
            for passage in range(passages):
                rows_ref[kind * blocks + block, passage * BLK : (passage + 1) * BLK] = held_ref[
                    kind, passage, block * BLK : (block + 1) * BLK
                ]
            rows_ref[kind * blocks + block, passages * BLK :] = named
        part = pl.ds(kind * blocks, blocks)
        outs.append(
            pltpu.make_async_copy(rows_ref.at[part], out_ref.at[part], out_sems.at[kind])
        )
        outs[kind].start()
    for copy in outs:
        copy.wait()


def pack(page_cache, own_ids, other_ids, early):
    passages, kinds, page_len, _ = page_cache.shape
    shape = (kinds * page_len // BLK, passages * BLK + IDS, HD)
    return pl.pallas_call(
        pack_kernel,
        out_shape=pltpu.HBM(shape, jnp.bfloat16),
        in_specs=[HBM, HBM, VMEM, HBM],
        out_specs=HBM,
        scratch_shapes=[
            pltpu.VMEM((kinds, passages, page_len, HD), jnp.bfloat16),
            pltpu.VMEM(own_ids.shape, own_ids.dtype),
            pltpu.VMEM(shape, jnp.bfloat16),
            pltpu.SemaphoreType.DMA((kinds,)),
            pltpu.SemaphoreType.DMA((kinds,)),
            pltpu.SemaphoreType.DMA((1,)),
        ],
        compiler_params=pltpu.CompilerParams(vmem_limit_bytes=FULL),
        cost_estimate=cost(0, 2 << 20),
        name="pack",
    )(in_hbm(page_cache), in_hbm(own_ids), other_ids, in_hbm(early))


def select_kernel(first_ref, held_ref, out_ref, chosen_ref, sems):
    dests, slots, pieces = out_ref.shape[:3]
    chunks = sems.shape[0]
    per = dests // chunks

    def copy_out(chunk):
        part = pl.ds(chunk * per, per)
        return pltpu.make_async_copy(chosen_ref.at[part], out_ref.at[part], sems.at[chunk])

    def fill(chunk, carry):
        for at in range(per):
            dest = chunk * per + at
            for slot in range(slots):
                chosen_ref[dest, slot] = held_ref[pl.ds(first_ref[dest, slot], pieces)]
        copy_out(chunk).start()
        return carry

    lax.fori_loop(0, chunks, fill, 0)
    for chunk in range(chunks):
        copy_out(chunk).wait()


def select(first, held, pieces):
    shape = first.shape + (pieces,) + held.shape[1:]
    return pl.pallas_call(
        select_kernel,
        out_shape=pltpu.HBM(shape, jnp.bfloat16),
        in_specs=[SMEM, VMEM],
        out_specs=HBM,
        scratch_shapes=[pltpu.VMEM(shape, jnp.bfloat16), pltpu.SemaphoreType.DMA((8,))],
        compiler_params=pltpu.CompilerParams(vmem_limit_bytes=12 << 20),
        cost_estimate=cost(0, 2 << 20),
        name="select",
    )(first, held)


def split_kernel(q_ref, k_ref, v_ref, kept_ref, sent_ref):
    rep = lax.axis_index("rep")
    width = q_ref.shape[2] // 2
    for chosen in range(2):

        @pl.when(rep == chosen)
        def _():
            for part, out_ref in ((chosen, kept_ref), (1 - chosen, sent_ref)):
                out_ref[:, :width] = q_ref[0, :, part * width : (part + 1) * width]
                out_ref[:, width : width + HD] = k_ref[0, :, part * HD : (part + 1) * HD]
                out_ref[:, width + HD :] = v_ref[0, :, part * HD : (part + 1) * HD]


def split_heads(queries, span_keys, span_values):
    tokens = queries.shape[1]
    width = queries.shape[2] // 2 + 2 * HD
    shape = jax.ShapeDtypeStruct((tokens, width), jnp.bfloat16)
    return pl.pallas_call(
        split_kernel,
        out_shape=(shape, shape),
        in_specs=[VMEM] * 3,
        out_specs=(VMEM, VMEM),
        compiler_params=pltpu.CompilerParams(vmem_limit_bytes=8 << 20),
        cost_estimate=cost(0, 2 << 20),
        name="split_heads",
    )(queries, span_keys, span_values)


def rope_kernel(kept_ref, got_ref, cos_ref, sin_ref, out_ref):
    heads = out_ref.shape[1] - 1
    for request, x_ref in enumerate((kept_ref, got_ref)):
        for part in range(heads):
            out_ref[request, part] = turn(
                x_ref[:, part * HD : (part + 1) * HD], cos_ref[request], sin_ref[request]
            )
        out_ref[request, heads] = x_ref[:, heads * HD :]


def rope_heads(kept, got, cosine, sine):
    tokens, width = kept.shape
    return pl.pallas_call(
        rope_kernel,
        out_shape=jax.ShapeDtypeStruct((2, width // HD, tokens, HD), jnp.bfloat16),
        in_specs=[VMEM] * 4,
        out_specs=VMEM,
        compiler_params=pltpu.CompilerParams(vmem_limit_bytes=8 << 20),
        cost_estimate=cost(0, 2 << 20),
        name="rope_heads",
    )(kept, got, cosine, sine)


def attention(span_ref, far_ref, block_ref, token_ref, out_ref, key_ref, request):
    heads = span_ref.shape[1] - 2
    tokens = span_ref.shape[2]
    far_len = key_ref.shape[0]
    blocks = far_ref.shape[0] // 2
    rows = GROUP * tokens
    shape = (GROUP, tokens, tokens)
    allowed = (
        lax.broadcasted_iota(jnp.int32, shape, 1) >= lax.broadcasted_iota(jnp.int32, shape, 2)
    ).reshape(rows, tokens)
    factor = math.log2(math.e) / math.sqrt(HD)
    contract = (((1,), (1,)), ((), ()))
    block_cos, block_sin = block_ref[0][:, None, :], block_ref[1][:, None, :]
    token_cos, token_sin = token_ref[0][None], token_ref[1][None]
    cosine = block_cos * token_cos - block_sin * token_sin
    sine = block_sin * token_cos + block_cos * token_sin
    key_ref[...] = turn(
        far_ref[:blocks, request].reshape(far_len, HD),
        cosine.reshape(far_len, HD),
        sine.reshape(far_len, HD),
    )

    def scores(first):
        q = span_ref[request, first : first + GROUP].reshape(rows, HD)
        far_s = lax.dot_general(q, key_ref[...], contract, preferred_element_type=jnp.float32)
        near_s = lax.dot_general(
            q, span_ref[request, heads], contract, preferred_element_type=jnp.float32
        )
        return far_s, jnp.where(allowed, near_s, -jnp.inf)

    def mix(first, far_s, near_s):
        row_max = jnp.maximum(
            jnp.max(far_s, axis=1, keepdims=True), jnp.max(near_s, axis=1, keepdims=True)
        )
        far_w = jnp.exp2((far_s - row_max) * factor)
        near_w = jnp.exp2((near_s - row_max) * factor)
        totals = jnp.sum(far_w, axis=1, keepdims=True) + jnp.sum(near_w, axis=1, keepdims=True)
        mixed = jnp.dot(
            far_w.astype(jnp.bfloat16),
            far_ref[blocks:, request].reshape(far_len, HD),
            preferred_element_type=jnp.float32,
        ) + jnp.dot(
            near_w.astype(jnp.bfloat16),
            span_ref[request, heads + 1],
            preferred_element_type=jnp.float32,
        )
        done = (mixed / totals).astype(jnp.bfloat16)
        for part in range(GROUP):
            out_ref[:, (first + part) * HD : (first + part + 1) * HD] = done[
                part * tokens : (part + 1) * tokens
            ]

    now = scores(0)
    for first in range(0, heads, GROUP):
        later = scores(first + GROUP) if first + GROUP < heads else None
        mix(first, *now)
        now = later


def fetch_weights(w_ref, out_refs, sems, shifts):
    blocks = w_ref.shape[1]
    rep, head = lax.axis_index("rep"), lax.axis_index("head")
    copies = []
    for at, (out_ref, shift) in enumerate(zip(out_refs, shifts)):
        width = out_ref.shape[2]
        block = lax.rem(head + jnp.where(rep == 0, shift[0], shift[1]), blocks)
        for part in range(2):
            for side, half in enumerate((rep, 1 - rep)):
                copy = pltpu.make_async_copy(
                    w_ref.at[part, block, pl.ds(pl.multiple_of(half * width, width), width)],
                    out_ref.at[part, side],
                    sems.at[at, part, side],
                )
                copy.start()
                copies.append(copy)
    return copies


def attention_kernel(span_ref, far_ref, block_ref, token_ref, w_ref, *refs, request, shifts):
    out_ref, *weight_refs, key_ref, sems = refs
    copies = fetch_weights(w_ref, weight_refs, sems, shifts)

    @pl.when(lax.axis_index("rep") >= 0)
    def _():
        attention(span_ref, far_ref, block_ref, token_ref, out_ref, key_ref, request)

    for copy in copies:
        copy.wait()


def attend(span, far, block_angles, token_angles, weights, request, shifts):
    _, parts, tokens, _ = span.shape
    heads = parts - 2
    far_len = block_angles.shape[1] * BLK
    _, _, rows, cols = weights.shape
    return pl.pallas_call(
        functools.partial(attention_kernel, request=request, shifts=shifts),
        out_shape=[jax.ShapeDtypeStruct((tokens, heads * HD), jnp.bfloat16)]
        + [pltpu.VMEM((2, 2, rows // 2, cols), weights.dtype)] * len(shifts),
        in_specs=[VMEM] * 4 + [HBM],
        out_specs=[VMEM] * (1 + len(shifts)),
        scratch_shapes=[
            pltpu.VMEM((far_len, HD), jnp.bfloat16),
            pltpu.SemaphoreType.DMA((len(shifts), 2, 2)),
        ],
        compiler_params=pltpu.CompilerParams(vmem_limit_bytes=FULL),
        cost_estimate=cost(
            4 * heads * tokens * (far_len + tokens) * HD,
            12 << 20,
            heads * tokens * (far_len + tokens),
        ),
        name=f"attend{request}",
    )(span, far, block_angles, token_angles, in_hbm(weights))


def regroup_part(raw_ref, out_ref, rows_ref, blocks_ref, sems, out_sems):
    slots, step = rows_ref.shape[:2]
    chunks = raw_ref.shape[0] // step

    def copy_in(chunk):
        part = pl.ds(pl.multiple_of(chunk * step, step), step)
        slot = chunk % slots
        return pltpu.make_async_copy(raw_ref.at[part], rows_ref.at[slot], sems.at[slot])

    def copy_out(chunk):
        part = pl.ds(pl.multiple_of(chunk * step, step), step)
        slot = chunk % slots
        return pltpu.make_async_copy(blocks_ref.at[slot], out_ref.at[:, part], out_sems.at[slot])

    for chunk in range(slots):
        copy_in(chunk).start()

    def move(chunk, carry):
        copy_in(chunk).wait()

        @pl.when(chunk >= slots)
        def _():
            copy_out(chunk - slots).wait()

        blocks_ref[chunk % slots] = jnp.swapaxes(rows_ref[chunk % slots], 0, 1)
        copy_out(chunk).start()

        @pl.when(chunk + slots < chunks)
        def _():
            copy_in(chunk + slots).start()

        return carry

    lax.fori_loop(0, chunks, move, 0)
    for chunk in range(chunks - slots, chunks):
        copy_out(chunk).wait()


def regroup_scratch(raw):
    rows, blocks, cols = raw.shape
    step, slots = rows // 16, 2
    return [
        pltpu.VMEM((slots, step, blocks, cols), raw.dtype),
        pltpu.VMEM((slots, blocks, step, cols), raw.dtype),
        pltpu.SemaphoreType.DMA((slots,)),
        pltpu.SemaphoreType.DMA((slots,)),
    ]


def regroup_early_kernel(own_ref, ids_ref, out_ref, *scratch):
    @pl.when(lax.axis_index("rep") == 1)
    def _():
        regroup_part(own_ref, out_ref.at[0], *scratch)


def regroup_early(own, ids):
    rows, blocks, cols = own.shape
    return pl.pallas_call(
        regroup_early_kernel,
        out_shape=pltpu.HBM((2, blocks, rows, cols), own.dtype),
        in_specs=[HBM, ANY],
        out_specs=HBM,
        scratch_shapes=regroup_scratch(own),
        compiler_params=pltpu.CompilerParams(vmem_limit_bytes=FULL),
        cost_estimate=cost(0, 16 << 20),
        name="regroup_early",
    )(in_hbm(own), ids)


def regroup_late_kernel(own_ref, other_ref, early_ref, out_ref, *scratch):
    @pl.when(lax.axis_index("rep") == 0)
    def _():
        regroup_part(own_ref, out_ref.at[0], *scratch)

    regroup_part(other_ref, out_ref.at[1], *scratch)


def regroup_late(own, other, early):
    return pl.pallas_call(
        regroup_late_kernel,
        out_shape=pltpu.HBM(early.shape, early.dtype),
        in_specs=[HBM] * 3,
        out_specs=HBM,
        input_output_aliases={2: 0},
        scratch_shapes=regroup_scratch(own),
        compiler_params=pltpu.CompilerParams(vmem_limit_bytes=FULL),
        cost_estimate=cost(0, 32 << 20),
        name="regroup_late",
    )(in_hbm(own), in_hbm(other), early)


def project_kernel(own_ref, other_ref, weight_ref, *refs):
    *more_refs, out_ref = refs
    rep = lax.axis_index("rep")
    cols = weight_ref.shape[3]
    for part, place in enumerate((rep, 1 - rep)):
        lanes = pl.ds(pl.multiple_of(place * cols, cols), cols)
        value = jnp.dot(
            own_ref[...], weight_ref[part, 0], preferred_element_type=jnp.float32
        ) + jnp.dot(other_ref[...], weight_ref[part, 1], preferred_element_type=jnp.float32)
        for more_ref in more_refs:
            value = value + more_ref[:, lanes].astype(jnp.float32)
        out_ref[:, lanes] = value.astype(out_ref.dtype)


def project(own, other, weight, dtype, name, *more):
    _, _, rows, cols = weight.shape
    tokens = own.shape[0]
    return pl.pallas_call(
        project_kernel,
        out_shape=jax.ShapeDtypeStruct((tokens, 2 * cols), dtype),
        in_specs=[VMEM] * (3 + len(more)),
        out_specs=VMEM,
        compiler_params=pltpu.CompilerParams(vmem_limit_bytes=FULL),
        cost_estimate=cost(8 * tokens * rows * cols, 4 << 20),
        name=name,
    )(own, other, weight, *more)


def on_device(queries, span_keys, span_values, page_cache, passage_ids, starts, out_weight):
    stores = lax.axis_size("store")
    head_count = lax.axis_size("head")
    per_store, _, page_len, _ = page_cache.shape
    pass_count = passage_ids.shape[1]
    tokens = queries.shape[1]
    page_blocks = page_len // BLK

    rep = lax.axis_index("rep")
    other_ids = lax.ppermute(passage_ids, "rep", SWAP)
    out_weight, _ = lax.optimization_barrier((out_weight, other_ids))
    raw = out_weight[:, :, 0, :]
    other_raw = lax.ppermute(raw, "rep", SWAP)
    early = regroup_early(raw, other_ids)
    packed = pack(page_cache, passage_ids, other_ids, early)
    held = lax.all_to_all(packed, "store", 0, 0, tiled=True)
    ids = held[:, per_store * BLK : per_store * BLK + 2, :pass_count].astype(jnp.int32)
    ids = jnp.where(rep == 0, ids, ids[:, ::-1]).reshape(2 * stores, pass_count)
    pieces = BLK // IDS
    first = ids // per_store * (per_store * pieces + 1) + ids % per_store * pieces
    chosen = select(first, held.reshape(-1, IDS, HD), pieces)
    chosen = chosen.reshape(stores, 2, pass_count, BLK, HD)

    weights = regroup_late(raw, other_raw, early)
    kept, sent = split_heads(queries, span_keys, span_values)
    got = lax.ppermute(sent, "rep", SWAP)
    begins = jnp.concatenate([starts, lax.ppermute(starts, "rep", SWAP)])
    query_pos = (
        jnp.min(begins, axis=1, keepdims=True)
        + pass_count * page_len
        + jnp.arange(tokens, dtype=jnp.int32)
    )
    span = rope_heads(kept, got, *angle_tables(query_pos))
    block_pos = jnp.arange(page_blocks, dtype=jnp.int32)[None, :, None] * BLK + begins[:, None, :]
    block_angles = jnp.stack(angle_tables(block_pos.reshape(2, -1)), axis=1)
    token_angles = jnp.stack(angle_tables(jnp.arange(BLK, dtype=jnp.int32)))

    far = lax.all_to_all(chosen, "store", 0, 0, tiled=True)

    other, opposite_w, plain_w = attend(
        span, far, block_angles[1], token_angles, weights, 1, ((2, 2), (3, 1))
    )
    other = lax.ppermute(other, "rep", SWAP)
    own, relayed_w, own_w = attend(
        span, far, block_angles[0], token_angles, weights, 0, ((1, 3), (0, 0))
    )

    ahead, behind = [], []
    for i in range(head_count):
        after, before = (i + 1) % head_count, (i - 1) % head_count
        ahead += [(2 * i, 2 * after), (2 * i + 1, 2 * before + 1)]
        behind += [(2 * i, 2 * before), (2 * i + 1, 2 * after + 1)]
    axes = ("head", "rep")
    opposite = project(own, other, opposite_w, jnp.bfloat16, "opposite")
    passing = lax.ppermute(opposite, axes, ahead)
    plain = project(own, other, plain_w, jnp.bfloat16, "plain")
    plain = lax.ppermute(plain, axes, behind)
    relayed = project(own, other, relayed_w, jnp.bfloat16, "relayed", passing)
    relayed = lax.ppermute(relayed, axes, ahead)
    total = project(own, other, own_w, jnp.float32, "kept")
    total = total + plain.astype(jnp.float32) + relayed.astype(jnp.float32)
    return total.astype(jnp.bfloat16)[None]


def solution(mesh):
    return jax.shard_map(
        on_device,
        mesh=mesh,
        in_specs=(
            P(("store", "rep"), None, "head"),
            P(("store", "rep"), None, "head"),
            P(("store", "rep"), None, "head"),
            P("store", None, None, "head"),
            P(("store", "rep"), None),
            P(("store", "rep"), None),
            P("head", None, "rep", None),
        ),
        out_specs=P(("store", "rep"), None, "head"),
        check_vma=False,
    )
```
